32 devices in a mesh: crop: 2 (over core), axial: 16 (over z, y, x).
Axes of the slice: x: 2, y: 2, z: 4, core: 2. Of those that a mesh axis runs over, the one named last changes fastest.
Arguments:
- pair: bfloat16 [2, 64, 64, 128], P('crop', 'axial'), may hold values from -6 to 6
- crop_mask: int32 [2, 64], P('crop'), may hold values 0 or 1
- weights: bfloat16 [128, 768], replicated, may hold values from -0.5 to 0.5
- probe_signs: int32 [128, 768], replicated, may hold values from 0 to 1
Outputs:
- pair_out: bfloat16 [2, 64, 64, 128], P('crop', 'axial')
- curvature: float32 [128, 768], replicated
The draws below stay inside these ranges and needn't reach their ends.
All inputs are finite; a program needn't handle non-finite values. No bound on the sum of `crop_mask` on one device may be relied on, other than what follows from the above.
Results may differ from the reference program's by a relative error of at most 0.006.
Values may be sent and summed in bfloat16 or wider, within the bound.
No kernel may reach another device: no remote copies, remote signals or barrier semaphores. Data moves between devices by JAX's collectives and lax.ppermute only.
A program may use at most 64 MiB of HBM per device.

```python
import jax
import jax.numpy as jnp
from jax import lax

C = 128
N = 64
CROPS = 2
WCOLS = 768


def place_ends(entries, own_key, smallest, top_value):
    spot = [jax.random.randint(jax.random.fold_in(own_key, axis), (), 0, length) for axis, length in enumerate(entries.shape)]
    longest = entries.shape.index(max(entries.shape))
    next_to = spot[:longest] + [(spot[longest] + 1) % entries.shape[longest]] + spot[longest + 1:]
    return entries.at[tuple(spot)].set(smallest).at[tuple(next_to)].set(top_value)


def level_of(stream_key, extent, cuts, low, top_value):
    level, own = 1.0, jax.random.fold_in(stream_key, 6)
    for position, blocks in cuts:
        heights = jnp.exp(jax.random.uniform(jax.random.fold_in(own, position), (blocks,), jnp.float32, low / len(cuts), top_value / len(cuts)))
        level = level * jnp.repeat(heights, extent[position] // blocks).reshape([-1 if axis == position else 1 for axis in range(len(extent))])
    return level


def normal_values(key, dims, spread, most, cuts=(), kind=jnp.bfloat16):
    factor_of = level_of(key, dims, cuts, -0.22, 0.18) if cuts else 1.0
    result = jax.random.normal(key, dims, jnp.float32) * spread * factor_of
    return jnp.minimum(jnp.maximum(result, -most), most).astype(kind)


def setup_inputs(seed: int = 0) -> dict:
    arg_keys = jax.random.split(jax.random.key(seed), 5)
    pair = normal_values(arg_keys[0], (CROPS, N, N, C), 1.0, 6.0, ((0, 2), (1, 16)))
    crop_mask = place_ends((jax.random.randint(arg_keys[1], (CROPS, N), 0, 8) < 7).astype(jnp.int32), jax.random.fold_in(arg_keys[1], 1), 0, 1)
    weights = normal_values(arg_keys[2], (C, WCOLS), C ** -0.5, 0.5)
    probe_signs = place_ends(jax.random.randint(arg_keys[3], (C, WCOLS), 0, 2), jax.random.fold_in(arg_keys[3], 1), 0, 1).astype(jnp.int32)
    return dict(pair=pair, crop_mask=crop_mask, weights=weights, probe_signs=probe_signs)


def norm_axis(value, axis):
    mean = lax.optimization_barrier(jnp.mean(value, axis=axis, keepdims=True))
    centered = value - mean
    var = lax.optimization_barrier(jnp.mean(centered * centered, axis=axis, keepdims=True))
    return centered * lax.rsqrt(var + 1e-05)

def project_in(w_in, zn_bf, mask_pair):
    proj = jnp.einsum('rnc,cd->drn', zn_bf.astype(jnp.float32), w_in.astype(jnp.bfloat16).astype(jnp.float32))
    hid = proj.shape[0] // 4
    a_full = jax.nn.sigmoid(proj[hid:2 * hid]) * proj[:hid] * mask_pair
    b_full = jax.nn.sigmoid(proj[3 * hid:]) * proj[2 * hid:3 * hid] * mask_pair
    return (a_full, b_full)

def head(w_head, x_full, zn_bf):
    chans = zn_bf.shape[2]
    w_gate = w_head[:, :chans].astype(jnp.bfloat16).astype(jnp.float32)
    w_out = w_head[:, chans:].astype(jnp.bfloat16).astype(jnp.float32)
    x_norm = norm_axis(x_full, 0).astype(jnp.bfloat16).astype(jnp.float32)
    out_proj = jnp.einsum('hrn,hc->rnc', x_norm, w_out)
    gating = jax.nn.sigmoid(jnp.einsum('rnc,cd->rnd', zn_bf.astype(jnp.float32), w_gate))
    return gating * out_proj

def tri_out(left, right):
    return jnp.einsum('cik,cjk->cij', left.astype(jnp.float32), right.astype(jnp.float32))

def one_crop(pair_crop, mask_crop, weights, probe_signs):
    chans = weights.shape[0]
    h4 = weights.shape[1] - 2 * chans
    zn = norm_axis(pair_crop.astype(jnp.float32), 2).astype(jnp.bfloat16)
    mask = mask_crop.astype(jnp.float32)
    mask_pair = mask[:, None] * mask[None, :]
    w_all = weights.astype(jnp.float32)
    probe = (2 * probe_signs - 1).astype(jnp.float32) * (1.0 / jnp.sqrt(jnp.float32(chans)))
    w_in, w_head = (w_all[:, :h4], w_all[:, h4:])
    v_in, v_head = (probe[:, :h4], probe[:, h4:])
    fin = lambda w: project_in(w, zn, mask_pair)
    (a_f, b_f), pull_in = jax.vjp(fin, w_in)
    _, (ta_f, tb_f) = jax.jvp(fin, (w_in,), (v_in,))
    a_bf, b_bf = (a_f.astype(jnp.bfloat16), b_f.astype(jnp.bfloat16))
    ta_bf, tb_bf = (ta_f.astype(jnp.bfloat16), tb_f.astype(jnp.bfloat16))
    x_bf = tri_out(a_bf, b_bf).astype(jnp.bfloat16)
    tx_bf = (tri_out(ta_bf, b_bf) + tri_out(a_bf, tb_bf)).astype(jnp.bfloat16)
    fhead = lambda w, xx: head(w, xx, zn)
    out, pull_head = jax.vjp(fhead, w_head, x_bf.astype(jnp.float32))
    _, t_out = jax.jvp(fhead, (w_head, x_bf.astype(jnp.float32)), (v_head, tx_bf.astype(jnp.float32)))
    total = CROPS * N * N
    cot = t_out * (1.0 / total)
    g_head, x_bar = pull_head(cot)
    xb_bf = x_bar.astype(jnp.bfloat16).astype(jnp.float32)
    a_bar = jnp.einsum('cij,cjk->cik', xb_bf, b_bf.astype(jnp.float32)).astype(jnp.bfloat16)
    b_bar = jnp.einsum('cij,cik->cjk', xb_bf, a_bf.astype(jnp.float32)).astype(jnp.bfloat16)
    g_in = pull_in((a_bar.astype(jnp.float32), b_bar.astype(jnp.float32)))[0]
    new_pair = (pair_crop.astype(jnp.float32) + out).astype(jnp.bfloat16)
    return (new_pair, jnp.concatenate([g_in, g_head], axis=1))

def reference(pair, crop_mask, weights, probe_signs):

    def step(items):
        return one_crop(items[0], items[1], weights, probe_signs)
    new_pairs, grads = lax.map(step, (pair, crop_mask))
    return (new_pairs, lax.optimization_barrier(jnp.sum(grads, axis=0)))
```

```python
import functools

import jax
import jax.numpy as jnp
import numpy as np
from jax import lax
from jax.experimental import pallas as pl
from jax.experimental.pallas import tpu as pltpu
from jax.sharding import PartitionSpec as P

BF = jnp.bfloat16
F32 = jnp.float32
VMEM = pl.BlockSpec(memory_space=pltpu.VMEM)
SMEM = pl.BlockSpec(memory_space=pltpu.SMEM)


def dot(left, right, dims=((1,), (0,))):
    return lax.dot_general(left, right, (dims, ((), ())), preferred_element_type=F32)


def log2(value):
    power = value.bit_length() - 1
    assert 1 << power == value
    return power


def centre(value):
    return value - jnp.mean(value, axis=1, keepdims=True)


def scale_of(centered):
    return lax.rsqrt(jnp.mean(centered * centered, axis=1, keepdims=True) + 1e-05)


def sigmoid(value):
    return 0.5 * jnp.tanh(0.5 * value) + 0.5


def block_kernel(cfg, place, mask_s, mask_v, w_ref, signs_ref, own_ref, *rest):
    g1, g2, rows, width, chans, total = cfg
    i_refs = (own_ref,) + rest[: g1 - 1]
    j_refs = (own_ref,) + rest[g1 - 1 : g1 + g2 - 2]
    (keep_ref, send_ref, y_ref, v_s, zi_s, zj_s, a_s, ta_s, sa_s, ga_s, b_s, tb_s, sb_s, gb_s,
     zp_s, px_s, pt_s, x_s, tx_s, xb_s, g_s) = rest[g1 + g2 - 2 :]
    n_i, n_j = g1 * rows, g2 * rows
    blk = rows * width
    me, core = place[0], place[1]
    unit = 1.0 / np.sqrt(np.float32(chans))
    v_s[...] = ((2 * signs_ref[...] - 1).astype(F32) * unit).astype(BF)

    def side(refs, step, first, z_s, val_s, tan_s, sig_s, gate_s):
        for m, ref in enumerate(refs):
            value = centre(ref[...].reshape(blk, chans).astype(F32))
            zn = (value * scale_of(value)).astype(BF)
            z_s[m * blk : (m + 1) * blk, :] = zn
            proj = dot(zn, w_ref[:, first : first + 2 * chans])
            tang = dot(zn, v_s[:, first : first + 2 * chans])
            base = jnp.bitwise_xor(me, m * step) * rows
            cover = jnp.concatenate(
                [mask_v[...] * mask_s[0, base + r].astype(F32) for r in range(rows)], axis=0
            )
            sig = sigmoid(proj[:, chans:])
            held = cover * sig
            val = held * proj[:, :chans]
            gate = val - val * sig
            here = slice(m * blk, (m + 1) * blk)
            val_s[here, :] = val
            tan_s[here, :] = held * tang[:, :chans] + gate * tang[:, chans:]
            sig_s[here, :] = held.astype(sig_s.dtype)
            gate_s[here, :] = gate.astype(gate_s.dtype)

    side(i_refs, 1, 0, zi_s, a_s, ta_s, sa_s, ga_s)
    side(j_refs, g1, 2 * chans, zj_s, b_s, tb_s, sb_s, gb_s)

    spot = lax.broadcasted_iota(jnp.int32, (n_j, width), 0)
    col = lax.broadcasted_iota(jnp.int32, (n_j, width), 1)
    owner = jnp.bitwise_xor(me, (spot >> log2(rows)) * g1)
    pick = jnp.where(col == owner * rows + (spot & (rows - 1)), 1.0, 0.0).astype(BF)
    for i in range(n_i):
        zp_s[i * n_j : (i + 1) * n_j, :] = dot(pick, zi_s[i * width : (i + 1) * width, :]).astype(BF)

    def fold(value):
        return jnp.sum(value.reshape(width // 8, 8, chans), axis=0)

    def tri(i, carry):
        at = pl.ds(pl.multiple_of(i * width, width), width)
        a, ta = a_s[at, :], ta_s[at, :]
        for j in range(n_j):
            here = slice(j * width, (j + 1) * width)
            b, tb = b_s[here, :], tb_s[here, :]
            to = pl.ds(pl.multiple_of(i * (n_j * 8), 8) + j * 8, 8)
            px_s[to, :] = fold(a * b)
            pt_s[to, :] = fold(ta * b + a * tb)
        return carry

    lax.fori_loop(0, n_i, tri, 0)
    pairs = n_i * n_j
    x_s[...] = sum(px_s[pl.ds(s, pairs, stride=8), :] for s in range(8)).astype(BF).astype(F32)
    tx_s[...] = sum(pt_s[pl.ds(s, pairs, stride=8), :] for s in range(8)).astype(BF).astype(F32)

    w_gate, w_out = w_ref[:, 4 * chans : 5 * chans], w_ref[:, 5 * chans :]
    v_gate, v_out = v_s[:, 4 * chans : 5 * chans], v_s[:, 5 * chans :]
    step = min(pairs, 256)
    for at in range(0, pairs, step):
        here = slice(at, at + step)
        zp = zp_s[here, :]
        xc = centre(x_s[here, :])
        inv = scale_of(xc)
        xhat = xc * inv
        xn = xhat.astype(BF)
        tc = centre(tx_s[here, :])
        txn = (inv * (tc - xhat * jnp.mean(xhat * tc, axis=1, keepdims=True))).astype(BF)
        out = dot(xn, w_out)
        t_out = dot(txn, w_out) + dot(xn, v_out)
        sig = sigmoid(dot(zp, w_gate))
        slope = sig * (1.0 - sig) * out
        y_ref[here, :] = (sig * out).astype(BF)
        bar = (sig * t_out + slope * dot(zp, v_gate)) * (1.0 / total)
        d_out = (bar * sig).astype(BF)
        d_gate = (bar * slope).astype(BF)
        part_gate = dot(zp, d_gate, ((0,), (0,)))
        part_out = dot(xn, d_out, ((0,), (0,)))
        if at == 0:
            g_s[1, chans : 2 * chans, :] = part_gate
            g_s[1, 2 * chans :, :] = part_out
        else:
            g_s[1, chans : 2 * chans, :] += part_gate
            g_s[1, 2 * chans :, :] += part_out
        dxn = dot(d_out, w_out, ((1,), (1,)))
        dc = centre(dxn)
        xb_s[here, :] = inv * (dc - xhat * jnp.mean(xhat * dxn, axis=1, keepdims=True))

    chunk = min(width, 64)

    def back(count, others, row_of, val_s, sig_s, gate_s, z_s, spots):
        def one(m, carry):
            bars = []
            for r in range(rows):
                for kc in range(0, width, chunk):
                    acc = None
                    for o in range(others):
                        row = xb_s[pl.ds(row_of(m * rows + r, o), 1), :]
                        term = row * val_s[o * width + kc : o * width + kc + chunk, :]
                        acc = term if acc is None else acc + term
                    bars.append(acc)
            at = pl.ds(pl.multiple_of(m * blk, blk), blk)
            bar = jnp.concatenate(bars, axis=0)
            both = jnp.concatenate(
                [(bar * sig_s[at, :].astype(F32)).astype(BF), (bar * gate_s[at, :].astype(F32)).astype(BF)], axis=1
            )
            part = dot(z_s[at, :], both, ((0,), (0,)))
            for n, (half, top) in enumerate(spots):
                g_s[half, top : top + chans, :] += part[:, n * chans : (n + 1) * chans]
            return carry

        for half, top in spots:
            g_s[half, top : top + chans, :] = jnp.zeros((chans, chans), F32)
        lax.fori_loop(0, count, one, 0)

    back(g1, n_j, lambda i, j: i * n_j + j, b_s, sa_s, ga_s, zi_s, ((0, 0), (0, chans)))
    back(g2, n_i, lambda j, i: i * n_j + j, a_s, sb_s, gb_s, zj_s, ((0, 2 * chans), (1, 0)))
    keep_ref[...] = g_s[core].astype(BF)
    send_ref[...] = g_s[1 - core].astype(BF)


def last_kernel(cfg, place, pair_ref, y_ref, mine_ref, other_ref, new_ref, curv_ref, g_s):
    g1, g2, rows, width, chans, _ = cfg
    me, core = place[0], place[1]
    n_j = g2 * rows
    col = lax.broadcasted_iota(jnp.int32, (width, width), 0)
    spot = lax.broadcasted_iota(jnp.int32, (width, width), 1)
    n = (spot >> log2(rows)) & (g2 - 1)
    owner = jnp.bitwise_xor(jnp.bitwise_xor(me, n * g1), spot >> log2(n_j))
    put = jnp.where(col == owner * rows + (spot & (rows - 1)), 1.0, 0.0).astype(BF)
    for r in range(rows):
        y = jnp.concatenate([y_ref[s, r * n_j : (r + 1) * n_j, :] for s in range(g1)], axis=0)
        new_ref[r] = (pair_ref[r].astype(F32) + dot(put, y)).astype(BF)
    g_s[core] = mine_ref[...].astype(F32)
    g_s[1 - core] = other_ref[...].astype(F32)
    for b in range(6):
        top = (b % 3) * chans
        curv_ref[:, b * chans : (b + 1) * chans] = g_s[b // 3, top : top + chans, :]


def shards(pair, crop_mask, weights, probe_signs):
    own = pair[0]
    rows, width, chans = own.shape
    n_axial, n_crop = lax.axis_size("axial"), lax.axis_size("crop")
    g1 = 1 << (log2(n_axial) // 2)
    g2 = n_axial // g1
    n_i, n_j = g1 * rows, g2 * rows
    cfg = (g1, g2, rows, width, chans, n_crop * width * width)

    def swap(value, axis, bit):
        return lax.ppermute(value, axis, [(i, i ^ bit) for i in range(lax.axis_size(axis))])

    along = [swap(own, "axial", m * g1) for m in range(1, g2)]
    plane = [swap(own, "axial", m) for m in range(1, g1)]
    place = jnp.stack([lax.axis_index("axial"), lax.axis_index("crop") & 1]).astype(jnp.int32)
    mask_v = jnp.broadcast_to(crop_mask[0].astype(F32)[:, None], (width, chans))
    kept = F32 if width <= 64 else BF
    wide = lambda n, dtype=F32: pltpu.VMEM((n * width, chans), dtype)
    half = jax.ShapeDtypeStruct((3 * chans, chans), BF)
    keep, send, y = pl.pallas_call(
        functools.partial(block_kernel, cfg),
        out_shape=(half, half, jax.ShapeDtypeStruct((n_i * n_j, chans), BF)),
        in_specs=[SMEM, SMEM] + [VMEM] * (2 + g1 + g2),
        out_specs=(VMEM, VMEM, VMEM),
        scratch_shapes=[
            pltpu.VMEM(weights.shape, BF),
            wide(n_i, BF), wide(n_j, BF),
            wide(n_i), wide(n_i), wide(n_i, kept), wide(n_i, kept),
            wide(n_j), wide(n_j), wide(n_j, kept), wide(n_j, kept),
            pltpu.VMEM((n_i * n_j, chans), BF),
            pltpu.VMEM((n_i * n_j * 8, chans), F32), pltpu.VMEM((n_i * n_j * 8, chans), F32),
            pltpu.VMEM((n_i * n_j, chans), F32), pltpu.VMEM((n_i * n_j, chans), F32),
            pltpu.VMEM((n_i * n_j, chans), F32),
            pltpu.VMEM((2, 3 * chans, chans), F32),
        ],
        compiler_params=pltpu.CompilerParams(vmem_limit_bytes=(40 if width <= 64 else 58) << 20),
        name="block",
    )(place, crop_mask, mask_v, weights, probe_signs, own, *plane, *along)

    def plus(one, two):
        return (one.astype(F32) + two.astype(F32)).astype(BF)

    g = plus(keep, swap(send, "crop", 1))
    bit = 2
    while bit < n_crop:
        g = plus(g, swap(g, "crop", bit))
        bit *= 2
    y = y.reshape(g1, 1, rows * n_j, chans)
    bit = 1
    while bit < g1:
        parts = y.reshape((y.shape[0] // 2, 2) + y.shape[1:])
        out = parts[:, 1].reshape(-1, chans)
        got = swap(jnp.concatenate([g, out], axis=0), "axial", bit)
        g = plus(g, got[: 3 * chans])
        y = jnp.concatenate([parts[:, 0], got[3 * chans :].reshape(parts[:, 1].shape)], axis=1)
        bit *= 2
    while bit < n_axial:
        g = plus(g, swap(g, "axial", bit))
        bit *= 2
    other = swap(g, "crop", 1)
    new_pair, curvature = pl.pallas_call(
        functools.partial(last_kernel, cfg),
        out_shape=(jax.ShapeDtypeStruct(own.shape, BF), jax.ShapeDtypeStruct(weights.shape, F32)),
        in_specs=[SMEM] + [VMEM] * 4,
        out_specs=(VMEM, VMEM),
        scratch_shapes=[pltpu.VMEM((2, 3 * chans, chans), F32)],
        compiler_params=pltpu.CompilerParams(vmem_limit_bytes=32 << 20),
        name="last",
    )(place, own, y[0], g, other)
    return (new_pair[None], curvature)


def solution(mesh):
    placed = (P("crop", "axial", None, None), P("crop", None), P(), P())
    return jax.shard_map(
        shards,
        mesh=mesh,
        in_specs=placed,
        out_specs=(P("crop", "axial", None, None), P()),
        check_vma=False,
    )
```

```python
import functools

import jax
import jax.numpy as jnp
import numpy as np
from jax import lax
from jax.experimental import pallas as pl
from jax.experimental.pallas import tpu as pltpu
from jax.sharding import PartitionSpec as P

BF = jnp.bfloat16
F32 = jnp.float32
VMEM = pl.BlockSpec(memory_space=pltpu.VMEM)
SMEM = pl.BlockSpec(memory_space=pltpu.SMEM)


def dot(left, right, dims=((1,), (0,))):
    return lax.dot_general(left, right, (dims, ((), ())), preferred_element_type=F32)


def log2(value):
    power = value.bit_length() - 1
    assert 1 << power == value
    return power


def centre(value):
    return value - jnp.mean(value, axis=1, keepdims=True)


def scale_of(centered):
    return lax.rsqrt(jnp.mean(centered * centered, axis=1, keepdims=True) + 1e-05)


def sigmoid(value):
    return 0.5 * jnp.tanh(0.5 * value) + 0.5


def flip(value, bits):
    return sum(((value >> b) & 1) << (bits - 1 - b) for b in range(bits))


def turned(core, value, bits):
    return jnp.where(core == 0, value, flip(value, bits))


def picker(cfg, place):
    g1, g2, rows, width, _, _ = cfg
    shape = (g2 * rows, width)
    spot = lax.broadcasted_iota(jnp.int32, shape, 0)
    col = lax.broadcasted_iota(jnp.int32, shape, 1)
    owner = jnp.bitwise_xor(place[0], turned(place[1], spot >> log2(rows), log2(g2)) * g1)
    return jnp.where(col == owner * rows + (spot & (rows - 1)), 1.0, 0.0).astype(BF)


def fill_side(cfg, place, mask_s, mask_v, w_ref, v_ref, blocks, step, first, outs):
    g1, g2, rows, width, chans, _ = cfg
    z_s, val_s, tan_s, sig_s, gate_s, *zp_s = outs
    if zp_s:
        pick = picker(cfg, place)
    blk = rows * width
    bits = log2(g1 if step == 1 else g2)
    for m, ref in blocks:
        here = slice(m * blk, (m + 1) * blk)
        value = centre(ref[...].reshape(blk, chans).astype(F32))
        zn = (value * scale_of(value)).astype(BF)
        z_s[:, here] = zn.T
        for r in range(rows if zp_s else 0):
            i = m * rows + r
            pairs = dot(pick, zn[r * width : (r + 1) * width]).astype(BF)
            zp_s[0][i * g2 * rows : (i + 1) * g2 * rows, :] = pairs
        proj = dot(zn, w_ref[:, first : first + 2 * chans])
        tang = dot(zn, v_ref[:, first : first + 2 * chans])
        base = jnp.bitwise_xor(place[0], turned(place[1], m, bits) * step) * rows
        cover = jnp.concatenate(
            [mask_v[...] * mask_s[0, base + r].astype(F32) for r in range(rows)], axis=0
        )
        sig = sigmoid(proj[:, chans:])
        held = cover * sig
        val = held * proj[:, :chans]
        gate = val - val * sig
        val_s[here, :] = val.astype(val_s.dtype)
        tan_s[here, :] = (held * tang[:, :chans] + gate * tang[:, chans:]).astype(tan_s.dtype)
        sig_s[here, :] = held.astype(sig_s.dtype)
        gate_s[here, :] = gate.astype(gate_s.dtype)


def own_kernel(cfg, place, mask_s, mask_v, w_ref, v_ref, own_ref, *outs):
    g1, chans = cfg[0], cfg[4]
    fill_side(cfg, place, mask_s, mask_v, w_ref, v_ref, [(0, own_ref)], 1, 0, outs[:6])
    fill_side(cfg, place, mask_s, mask_v, w_ref, v_ref, [(0, own_ref)], g1, 2 * chans, outs[6:])


def rows_kernel(cfg, place, mask_s, mask_v, w_ref, v_ref, *rest):
    g1, g2, chans = cfg[0], cfg[1], cfg[4]
    count = g1 + g2 - 3
    refs, outs = rest[:count], rest[count + 11 :]
    fill_side(cfg, place, mask_s, mask_v, w_ref, v_ref,
              [(m + 1, refs[g1 - 2 + m]) for m in range(g2 - 1)], g1, 2 * chans, outs[6:])
    fill_side(cfg, place, mask_s, mask_v, w_ref, v_ref,
              [(m + 2, refs[m]) for m in range(g1 - 2)], 1, 0, outs[:6])


def block_kernel(cfg, place, mask_s, mask_v, w_ref, v_s, zj_s, b_s, tb_s, sb_s, gb_s, late_ref, *rest):
    g1, g2, rows, width, chans, total = cfg
    (keep_ref, send_ref, y_ref, zi_s, a_s, ta_s, sa_s, ga_s, zp_s,
     px_s, pt_s, x_s, tx_s, xb_s, d_s, g_s) = rest[6:]
    n_i, n_j = g1 * rows, g2 * rows
    blk = rows * width
    core = place[1]
    fill_side(cfg, place, mask_s, mask_v, w_ref, v_s, [(1, late_ref)], 1, 0,
              (zi_s, a_s, ta_s, sa_s, ga_s, zp_s))

    def fold(value):
        return jnp.sum(value.reshape(width // 8, 8, chans), axis=0)

    def tri(i, carry):
        at = pl.ds(pl.multiple_of(i * width, width), width)
        a, ta = a_s[at, :].astype(F32), ta_s[at, :].astype(F32)
        for j in range(n_j):
            here = slice(j * width, (j + 1) * width)
            b, tb = b_s[here, :].astype(F32), tb_s[here, :].astype(F32)
            to = pl.ds(pl.multiple_of(i * (n_j * 8), 8) + j * 8, 8)
            px_s[to, :] = fold(a * b)
            pt_s[to, :] = fold(ta * b + a * tb)
        return carry

    lax.fori_loop(0, n_i, tri, 0)
    pairs = n_i * n_j
    x_s[...] = sum(px_s[pl.ds(s, pairs, stride=8), :] for s in range(8)).astype(BF).astype(F32)
    tx_s[...] = sum(pt_s[pl.ds(s, pairs, stride=8), :] for s in range(8)).astype(BF).astype(F32)

    w_gate, w_out = w_ref[:, 4 * chans : 5 * chans], w_ref[:, 5 * chans :]
    v_gate, v_out = v_s[:, 4 * chans : 5 * chans], v_s[:, 5 * chans :]
    step = min(pairs, 256)
    for at in range(0, pairs, step):
        here = slice(at, at + step)
        zp = zp_s[here, :]
        xc = centre(x_s[here, :])
        inv = scale_of(xc)
        xhat = xc * inv
        xn = xhat.astype(BF)
        tc = centre(tx_s[here, :])
        txn = (inv * (tc - xhat * jnp.mean(xhat * tc, axis=1, keepdims=True))).astype(BF)
        out = dot(xn, w_out)
        t_out = dot(txn, w_out) + dot(xn, v_out)
        sig = sigmoid(dot(zp, w_gate))
        slope = sig * (1.0 - sig) * out
        y_ref[here, :] = (sig * out).astype(BF)
        bar = (sig * t_out + slope * dot(zp, v_gate)) * (1.0 / total)
        d_out = (bar * sig).astype(BF)
        d_gate = (bar * slope).astype(BF)
        part_gate = dot(zp, d_gate, ((0,), (0,)))
        part_out = dot(xn, d_out, ((0,), (0,)))
        if at == 0:
            g_s[1, chans : 2 * chans, :] = part_gate
            g_s[1, 2 * chans :, :] = part_out
        else:
            g_s[1, chans : 2 * chans, :] += part_gate
            g_s[1, 2 * chans :, :] += part_out
        dxn = dot(d_out, w_out, ((1,), (1,)))
        dc = centre(dxn)
        xb_s[here, :] = inv * (dc - xhat * jnp.mean(xhat * dxn, axis=1, keepdims=True))

    chunk = min(width, 64)

    def back(count, others, row_of, val_s, sig_s, gate_s, z_s, spots):
        def one(m, carry):
            bars = []
            for r in range(rows):
                for kc in range(0, width, chunk):
                    acc = None
                    for o in range(others):
                        row = xb_s[pl.ds(row_of(m * rows + r, o), 1), :]
                        term = row * val_s[o * width + kc : o * width + kc + chunk, :].astype(F32)
                        acc = term if acc is None else acc + term
                    bars.append(acc)
            at = pl.ds(pl.multiple_of(m * blk, blk), blk)
            bar = jnp.concatenate(bars, axis=0)
            d_s[at, :chans] = (bar * sig_s[at, :].astype(F32)).astype(BF)
            d_s[at, chans:] = (bar * gate_s[at, :].astype(F32)).astype(BF)
            return carry

        lax.fori_loop(0, count, one, 0)
        part = dot(z_s[...], d_s[: count * blk, :])
        for n, (half, top) in enumerate(spots):
            g_s[half, top : top + chans, :] = part[:, n * chans : (n + 1) * chans]

    back(g1, n_j, lambda i, j: i * n_j + j, b_s, sa_s, ga_s, zi_s, ((0, 0), (0, chans)))
    back(g2, n_i, lambda j, i: i * n_j + j, a_s, sb_s, gb_s, zj_s, ((0, 2 * chans), (1, 0)))
    keep_ref[...] = g_s[core].astype(BF)
    send_ref[...] = g_s[1 - core].astype(BF)


def pair_kernel(cfg, place, pair_ref, y_ref, new_ref):
    g1, g2, rows, width, _, _ = cfg
    me, core = place[0], place[1]
    n_j = g2 * rows
    col = lax.broadcasted_iota(jnp.int32, (width, width), 0)
    spot = lax.broadcasted_iota(jnp.int32, (width, width), 1)
    n = turned(core, (spot >> log2(rows)) & (g2 - 1), log2(g2))
    s = turned(core, spot >> log2(n_j), log2(g1))
    owner = jnp.bitwise_xor(jnp.bitwise_xor(me, n * g1), s)
    put = jnp.where(col == owner * rows + (spot & (rows - 1)), 1.0, 0.0).astype(BF)
    for r in range(rows):
        y = jnp.concatenate([y_ref[s, r * n_j : (r + 1) * n_j, :] for s in range(g1)], axis=0)
        new_ref[r] = (pair_ref[r].astype(F32) + dot(put, y)).astype(BF)


def last_kernel(cfg, place, mine_ref, other_ref, curv_ref, g_s):
    chans = cfg[4]
    core = place[1]
    g_s[core] = mine_ref[...].astype(F32)
    g_s[1 - core] = other_ref[...].astype(F32)
    for b in range(6):
        top = (b % 3) * chans
        curv_ref[:, b * chans : (b + 1) * chans] = g_s[b // 3, top : top + chans, :]


def shards(pair, crop_mask, weights, probe_signs):
    own = pair[0]
    rows, width, chans = own.shape
    n_axial, n_crop = lax.axis_size("axial"), lax.axis_size("crop")
    g1 = 1 << (log2(n_axial) // 2)
    g2 = n_axial // g1
    n_i, n_j = g1 * rows, g2 * rows
    cfg = (g1, g2, rows, width, chans, n_crop * width * width)

    def crop_swap(value, bit):
        return lax.ppermute(value, "crop", [(i, i ^ bit) for i in range(n_crop)])

    def swap(value, m, step, mixed=True):
        bits = log2(g1 if step == 1 else g2)
        pairs = []
        for q in range(n_crop):
            there = (flip(m, bits) if mixed and q & 1 else m) * step
            pairs += [(q * n_axial + i, q * n_axial + (i ^ there)) for i in range(n_axial)]
        return lax.ppermute(value, ("crop", "axial"), pairs)

    along = [swap(own, m, g1) for m in range(1, g2)]
    plane = [swap(own, m, 1) for m in range(2, g1)]
    place = jnp.stack([lax.axis_index("axial"), lax.axis_index("crop") & 1]).astype(jnp.int32)
    mask_v = jnp.broadcast_to(crop_mask[0].astype(F32)[:, None], (width, chans))
    kept = F32 if width <= 64 else BF
    shape = jax.ShapeDtypeStruct
    pairs = (n_i * n_j, chans)
    side = lambda n: [shape((chans, n * width), BF)] + [shape((n * width, chans), t) for t in (kept,) * 4]
    side_a, side_b = side(n_i) + [shape(pairs, BF)], side(n_j)
    half = shape((3 * chans, chans), BF)
    params = lambda: pltpu.CompilerParams(vmem_limit_bytes=(40 if width <= 64 else 58) << 20)
    cost = lambda us: pl.CostEstimate(flops=int(us * 1e9), bytes_accessed=0, transcendentals=0)

    unit = 1.0 / np.sqrt(np.float32(chans))
    v = ((2 * probe_signs - 1).astype(F32) * unit).astype(BF)
    later, along[-1], v = lax.optimization_barrier((own, along[-1], v))
    late = swap(later, 1, 1)
    sides = pl.pallas_call(
        functools.partial(own_kernel, cfg),
        out_shape=side_a + side_b,
        in_specs=[SMEM, SMEM] + [VMEM] * 4,
        out_specs=[VMEM] * 11,
        compiler_params=params(),
        cost_estimate=cost(0.01),
        name="own_rows",
    )(place, crop_mask, mask_v, weights, v, own)
    sides = pl.pallas_call(
        functools.partial(rows_kernel, cfg),
        out_shape=side_a + side_b,
        in_specs=[SMEM, SMEM] + [VMEM] * (3 + g1 + g2 - 3 + 11),
        out_specs=[VMEM] * 11,
        input_output_aliases={2 + g1 + g2 + i: i for i in range(11)},
        compiler_params=params(),
        cost_estimate=cost(0.01),
        name="rows",
    )(place, crop_mask, mask_v, weights, v, *plane, *along, *sides)
    keep, send, y, *_ = pl.pallas_call(
        functools.partial(block_kernel, cfg),
        out_shape=[half, half, shape(pairs, BF)] + side_a,
        in_specs=[SMEM, SMEM] + [VMEM] * 15,
        out_specs=[VMEM] * 9,
        input_output_aliases={11 + i: 3 + i for i in range(6)},
        scratch_shapes=[pltpu.VMEM((pairs[0] * 8, chans), F32)] * 2
        + [pltpu.VMEM(pairs, F32)] * 3
        + [pltpu.VMEM((max(n_i, n_j) * width, 2 * chans), BF)]
        + [pltpu.VMEM((2, 3 * chans, chans), F32)],
        compiler_params=params(),
        cost_estimate=cost(5.0),
        name="block",
    )(place, crop_mask, mask_v, weights, v, *sides[6:], late, *sides[:6])

    def plus(one, two):
        return (one.astype(F32) + two.astype(F32)).astype(BF)

    g = plus(keep, crop_swap(send, 1))
    bit = 2
    while bit < n_crop:
        g = plus(g, crop_swap(g, bit))
        bit *= 2
    y = y.reshape(g1, 1, rows * n_j, chans)
    bit = 1
    while bit < g1:
        parts = y.reshape((y.shape[0] // 2, 2) + y.shape[1:])
        out = parts[:, 1].reshape(-1, chans)
        got = swap(jnp.concatenate([g, out], axis=0), bit, 1)
        g = plus(g, got[: 3 * chans])
        y = jnp.concatenate([parts[:, 0], got[3 * chans :].reshape(parts[:, 1].shape)], axis=1)
        bit *= 2
    new_pair = pl.pallas_call(
        functools.partial(pair_kernel, cfg),
        out_shape=shape(own.shape, BF),
        in_specs=[SMEM] + [VMEM] * 2,
        out_specs=VMEM,
        compiler_params=params(),
        cost_estimate=cost(0.5),
        name="new_pair",
    )(place, own, y[0])
    bit = 1
    while bit < g2:
        g = plus(g, swap(g, bit, g1, False))
        g, new_pair = lax.optimization_barrier((g, new_pair))
        bit *= 2
    curvature = pl.pallas_call(
        functools.partial(last_kernel, cfg),
        out_shape=shape(weights.shape, F32),
        in_specs=[SMEM] + [VMEM] * 2,
        out_specs=VMEM,
        scratch_shapes=[pltpu.VMEM((2, 3 * chans, chans), F32)],
        compiler_params=params(),
        cost_estimate=cost(0.5),
        name="halves",
    )(place, g, crop_swap(g, 1))
    return (new_pair[None], curvature)


def solution(mesh):
    placed = (P("crop", "axial", None, None), P("crop", None), P(), P())
    return jax.shard_map(
        shards,
        mesh=mesh,
        in_specs=placed,
        out_specs=(P("crop", "axial", None, None), P()),
        check_vma=False,
    )
```

```python
import functools

import jax
import jax.numpy as jnp
import numpy as np
from jax import lax
from jax.experimental import pallas as pl
from jax.experimental.pallas import tpu as pltpu
from jax.sharding import PartitionSpec as P

BF = jnp.bfloat16
F32 = jnp.float32
VMEM = pl.BlockSpec(memory_space=pltpu.VMEM)
ANY = pl.BlockSpec(memory_space=pl.ANY)
SMEM = pl.BlockSpec(memory_space=pltpu.SMEM)


def dot(left, right, dims=((1,), (0,))):
    return lax.dot_general(left, right, (dims, ((), ())), preferred_element_type=F32)


def log2(value):
    power = value.bit_length() - 1
    assert 1 << power == value
    return power


def centre(value):
    return value - jnp.mean(value, axis=1, keepdims=True)


def scale_of(centered):
    return lax.rsqrt(jnp.mean(centered * centered, axis=1, keepdims=True) + 1e-05)


def sigmoid(value):
    return 0.5 * jnp.tanh(0.5 * value) + 0.5


def flip(value, bits):
    return sum(((value >> b) & 1) << (bits - 1 - b) for b in range(bits))


def turned(core, value, bits):
    return jnp.where(core == 0, value, flip(value, bits))


def picker(cfg, place):
    g1, g2, rows, width, _, _ = cfg
    shape = (g2 * rows, width)
    spot = lax.broadcasted_iota(jnp.int32, shape, 0)
    col = lax.broadcasted_iota(jnp.int32, shape, 1)
    owner = jnp.bitwise_xor(place[0], turned(place[1], spot >> log2(rows), log2(g2)) * g1)
    return jnp.where(col == owner * rows + (spot & (rows - 1)), 1.0, 0.0).astype(BF)


def fill_side(cfg, place, mask_s, mask_v, w_ref, v_ref, blocks, step, first, outs):
    g1, g2, rows, width, chans, _ = cfg
    z_s, val_s, tan_s, sig_s, gate_s, *zp_s = outs
    if zp_s:
        pick = picker(cfg, place)
    blk = rows * width
    bits = log2(g1 if step == 1 else g2)
    for m, ref in blocks:
        here = slice(m * blk, (m + 1) * blk)
        value = centre(ref[...].reshape(blk, chans).astype(F32))
        zn = (value * scale_of(value)).astype(BF)
        z_s[:, here] = zn.T
        for r in range(rows if zp_s else 0):
            i = m * rows + r
            pairs = dot(pick, zn[r * width : (r + 1) * width]).astype(BF)
            zp_s[0][i * g2 * rows : (i + 1) * g2 * rows, :] = pairs
        proj = dot(zn, w_ref[:, first : first + 2 * chans])
        tang = dot(zn, v_ref[:, first : first + 2 * chans])
        base = jnp.bitwise_xor(place[0], turned(place[1], m, bits) * step) * rows
        cover = jnp.concatenate(
            [mask_v[...] * mask_s[0, base + r].astype(F32) for r in range(rows)], axis=0
        )
        sig = sigmoid(proj[:, chans:])
        held = cover * sig
        val = held * proj[:, :chans]
        gate = val - val * sig
        val_s[here, :] = val.astype(val_s.dtype)
        tan_s[here, :] = (held * tang[:, :chans] + gate * tang[:, chans:]).astype(tan_s.dtype)
        sig_s[here, :] = held.astype(sig_s.dtype)
        gate_s[here, :] = gate.astype(gate_s.dtype)


def own_kernel(cfg, place, mask_s, mask_v, w_ref, v_ref, own_ref, *outs):
    g1, chans = cfg[0], cfg[4]
    fill_side(cfg, place, mask_s, mask_v, w_ref, v_ref, [(0, own_ref)], 1, 0, outs[:6])
    fill_side(cfg, place, mask_s, mask_v, w_ref, v_ref, [(0, own_ref)], g1, 2 * chans, outs[6:])


def triangle(cfg, first, count, a_s, ta_s, b_s, tb_s, px_s, pt_s, x_ref, tx_ref):
    _, g2, rows, width, chans, _ = cfg
    n_j = g2 * rows

    def fold(value):
        return jnp.sum(value.reshape(width // 8, 8, chans), axis=0)

    def tri(i, carry):
        at = pl.ds(pl.multiple_of((first + i) * width, width), width)
        a, ta = a_s[at, :].astype(F32), ta_s[at, :].astype(F32)
        for j in range(n_j):
            here = slice(j * width, (j + 1) * width)
            b, tb = b_s[here, :].astype(F32), tb_s[here, :].astype(F32)
            to = pl.ds(pl.multiple_of(i * (n_j * 8), 8) + j * 8, 8)
            px_s[to, :] = fold(a * b)
            pt_s[to, :] = fold(ta * b + a * tb)
        return carry

    lax.fori_loop(0, count, tri, 0, unroll=2 if width <= 64 else 1)
    pairs = count * n_j
    here = slice(first * n_j, (first + count) * n_j)
    for part, out in ((px_s, x_ref), (pt_s, tx_ref)):
        total = sum(part[pl.ds(s, pairs, stride=8), :] for s in range(8))
        out[here, :] = total.astype(BF).astype(F32)


def line_kernel(cfg, place, mask_s, mask_v, w_ref, v_ref, a_s, ta_s, *rest):
    g1, g2, rows, width, chans, _ = cfg
    refs, (*outs, x_ref, tx_ref, px_s, pt_s) = rest[: g2 - 1], rest[g2 + 4 :]
    fill_side(cfg, place, mask_s, mask_v, w_ref, v_ref,
              [(m + 1, refs[m]) for m in range(g2 - 1)], g1, 2 * chans, outs)
    triangle(cfg, 0, rows, a_s, ta_s, outs[1], outs[2], px_s, pt_s, x_ref, tx_ref)


def block_kernel(cfg, place, mask_s, mask_v, w_ref, v_s, zj_s, b_s, tb_s, sb_s, gb_s, x_in, tx_in, *rest):
    g1, g2, rows, width, chans, total = cfg
    refs = rest[: g1 - 1]
    (keep_ref, send_ref, y_ref, zi_s, a_s, ta_s, sa_s, ga_s, zp_s,
     px_s, pt_s, x_s, tx_s, xb_s, d_s, g_s) = rest[g1 + 5 :]
    n_i, n_j = g1 * rows, g2 * rows
    blk = rows * width
    core = place[1]
    fill_side(cfg, place, mask_s, mask_v, w_ref, v_s,
              [(m, refs[m - 1]) for m in range(g1 - 1, 0, -1)], 1, 0, (zi_s, a_s, ta_s, sa_s, ga_s, zp_s))
    x_s[: rows * n_j, :] = x_in[...]
    tx_s[: rows * n_j, :] = tx_in[...]
    triangle(cfg, rows, n_i - rows, a_s, ta_s, b_s, tb_s, px_s, pt_s, x_s, tx_s)
    pairs = n_i * n_j

    w_gate, w_out = w_ref[:, 4 * chans : 5 * chans], w_ref[:, 5 * chans :]
    v_gate, v_out = v_s[:, 4 * chans : 5 * chans], v_s[:, 5 * chans :]
    step = min(pairs, 256)
    for at in range(0, pairs, step):
        here = slice(at, at + step)
        zp = zp_s[here, :]
        xc = centre(x_s[here, :])
        inv = scale_of(xc)
        xhat = xc * inv
        xn = xhat.astype(BF)
        tc = centre(tx_s[here, :])
        txn = (inv * (tc - xhat * jnp.mean(xhat * tc, axis=1, keepdims=True))).astype(BF)
        out = dot(xn, w_out)
        t_out = dot(txn, w_out) + dot(xn, v_out)
        sig = sigmoid(dot(zp, w_gate))
        slope = sig * (1.0 - sig) * out
        y_ref[here, :] = (sig * out).astype(BF)
        bar = (sig * t_out + slope * dot(zp, v_gate)) * (1.0 / total)
        d_out = (bar * sig).astype(BF)
        d_gate = (bar * slope).astype(BF)
        part_gate = dot(zp, d_gate, ((0,), (0,)))
        part_out = dot(xn, d_out, ((0,), (0,)))
        if at == 0:
            g_s[1, chans : 2 * chans, :] = part_gate
            g_s[1, 2 * chans :, :] = part_out
        else:
            g_s[1, chans : 2 * chans, :] += part_gate
            g_s[1, 2 * chans :, :] += part_out
        dxn = dot(d_out, w_out, ((1,), (1,)))
        dc = centre(dxn)
        xb_s[here, :] = inv * (dc - xhat * jnp.mean(xhat * dxn, axis=1, keepdims=True))

    chunk = min(width, 64)

    def back(count, others, row_of, val_s, sig_s, gate_s, z_s, spots):
        def one(m, carry):
            bars = [[] for _ in range(rows)]
            for kc in range(0, width, chunk):
                sums = [None] * rows
                for o in range(others):
                    val = val_s[o * width + kc : o * width + kc + chunk, :].astype(F32)
                    for r in range(rows):
                        term = xb_s[pl.ds(row_of(m * rows + r, o), 1), :] * val
                        sums[r] = term if o == 0 else sums[r] + term
                for r in range(rows):
                    bars[r].append(sums[r])
            bars = sum(bars, [])
            at = pl.ds(pl.multiple_of(m * blk, blk), blk)
            bar = jnp.concatenate(bars, axis=0)
            d_s[at, :chans] = (bar * sig_s[at, :].astype(F32)).astype(BF)
            d_s[at, chans:] = (bar * gate_s[at, :].astype(F32)).astype(BF)
            return carry

        lax.fori_loop(0, count, one, 0, unroll=width <= 64)
        part = dot(z_s[...], d_s[: count * blk, :])
        for n, (half, top) in enumerate(spots):
            g_s[half, top : top + chans, :] = part[:, n * chans : (n + 1) * chans]

    back(g1, n_j, lambda i, j: i * n_j + j, b_s, sa_s, ga_s, zi_s, ((0, 0), (0, chans)))
    back(g2, n_i, lambda j, i: i * n_j + j, a_s, sb_s, gb_s, zj_s, ((0, 2 * chans), (1, 0)))
    keep_ref[...] = g_s[core].astype(BF)
    send_ref[...] = g_s[1 - core].astype(BF)


def pair_kernel(cfg, place, pair_ref, y_ref, new_ref):
    g1, g2, rows, width, _, _ = cfg
    me, core = place[0], place[1]
    n_j = g2 * rows
    col = lax.broadcasted_iota(jnp.int32, (width, width), 0)
    spot = lax.broadcasted_iota(jnp.int32, (width, width), 1)
    n = turned(core, (spot >> log2(rows)) & (g2 - 1), log2(g2))
    s = turned(core, spot >> log2(n_j), log2(g1))
    owner = jnp.bitwise_xor(jnp.bitwise_xor(me, n * g1), s)
    put = jnp.where(col == owner * rows + (spot & (rows - 1)), 1.0, 0.0).astype(BF)
    for r in range(rows):
        y = jnp.concatenate([y_ref[s, r * n_j : (r + 1) * n_j, :] for s in range(g1)], axis=0)
        new_ref[r] = (pair_ref[r].astype(F32) + dot(put, y)).astype(BF)


def shards(pair, crop_mask, weights, probe_signs):
    own = pair[0]
    rows, width, chans = own.shape
    n_axial, n_crop = lax.axis_size("axial"), lax.axis_size("crop")
    g1 = 1 << (log2(n_axial) // 2)
    g2 = n_axial // g1
    n_i, n_j = g1 * rows, g2 * rows
    cfg = (g1, g2, rows, width, chans, n_crop * width * width)

    def crop_swap(value, bit):
        return lax.ppermute(value, "crop", [(i, i ^ bit) for i in range(n_crop)])

    def swap(value, m, step, mixed=True):
        bits = log2(g1 if step == 1 else g2)
        pairs = []
        for q in range(n_crop):
            there = (flip(m, bits) if mixed and q & 1 else m) * step
            pairs += [(q * n_axial + i, q * n_axial + (i ^ there)) for i in range(n_axial)]
        return lax.ppermute(value, ("crop", "axial"), pairs)

    along = [swap(own, m, g1) for m in range(1, g2)]
    place = jnp.stack([lax.axis_index("axial"), lax.axis_index("crop") & 1]).astype(jnp.int32)
    mask_v = jnp.broadcast_to(crop_mask[0].astype(F32)[:, None], (width, chans))
    kept = F32 if width <= 64 else BF
    shape = jax.ShapeDtypeStruct
    pairs = (n_i * n_j, chans)
    side = lambda n: [shape((chans, n * width), BF)] + [shape((n * width, chans), t) for t in (kept,) * 4]
    side_a, side_b = side(n_i) + [shape(pairs, BF)], side(n_j)
    half = shape((3 * chans, chans), BF)
    params = lambda: pltpu.CompilerParams(vmem_limit_bytes=(40 if width <= 64 else 58) << 20)
    cost = lambda us: pl.CostEstimate(flops=int(us * 1e9), bytes_accessed=0, transcendentals=0)

    unit = 1.0 / np.sqrt(np.float32(chans))
    v = ((2 * probe_signs - 1).astype(F32) * unit).astype(BF)
    later, v = lax.optimization_barrier((own, v))
    plane = [swap(later, m, 1) for m in range(1, g1)]
    sides = pl.pallas_call(
        functools.partial(own_kernel, cfg),
        out_shape=side_a + side_b,
        in_specs=[SMEM, SMEM] + [VMEM] * 4,
        out_specs=[VMEM] * 11,
        compiler_params=params(),
        cost_estimate=cost(0.01),
        name="own_rows",
    )(place, crop_mask, mask_v, weights, v, own)
    own_pairs = shape((rows * n_j, chans), F32)
    part = pltpu.VMEM((rows * n_j * 8, chans), F32)
    *line, x, tx = pl.pallas_call(
        functools.partial(line_kernel, cfg),
        out_shape=side_b + [own_pairs, own_pairs],
        in_specs=[SMEM, SMEM] + [VMEM] * (5 + g2 - 1 + 5),
        out_specs=[VMEM] * 7,
        input_output_aliases={6 + g2 + i: i for i in range(5)},
        scratch_shapes=[part, part],
        compiler_params=params(),
        cost_estimate=cost(0.01),
        name="line",
    )(place, crop_mask, mask_v, weights, v, sides[1], sides[2], *along, *sides[6:])
    part = pltpu.VMEM(((n_i - rows) * n_j * 8, chans), F32)
    keep, send, y, *_ = pl.pallas_call(
        functools.partial(block_kernel, cfg),
        out_shape=[half, half, shape(pairs, BF)] + side_a,
        in_specs=[SMEM, SMEM] + [VMEM] * (10 + g1 - 1 + 6),
        out_specs=[VMEM] * 9,
        input_output_aliases={11 + g1 + i: 3 + i for i in range(6)},
        scratch_shapes=[part, part]
        + [pltpu.VMEM(pairs, F32)] * 3
        + [pltpu.VMEM((max(n_i, n_j) * width, 2 * chans), BF)]
        + [pltpu.VMEM((2, 3 * chans, chans), F32)],
        compiler_params=params(),
        cost_estimate=cost(5.0),
        name="block",
    )(place, crop_mask, mask_v, weights, v, *line, x, tx, *plane, *sides[:6])

    def plus(one, two):
        return (one.astype(F32) + two.astype(F32)).astype(BF)

    g = plus(keep, crop_swap(send, 1))
    bit = 2
    while bit < n_crop:
        g = plus(g, crop_swap(g, bit))
        bit *= 2
    y = y.reshape(g1, 1, rows * n_j, chans)
    bit = 1
    while bit < g1:
        parts = y.reshape((y.shape[0] // 2, 2) + y.shape[1:])
        out = parts[:, 1].reshape(-1, chans)
        got = swap(jnp.concatenate([g, out], axis=0), bit, 1)
        g = plus(g, got[: 3 * chans])
        y = jnp.concatenate([parts[:, 0], got[3 * chans :].reshape(parts[:, 1].shape)], axis=1)
        bit *= 2
    new_pair = pl.pallas_call(
        functools.partial(pair_kernel, cfg),
        out_shape=shape(own.shape, BF),
        in_specs=[SMEM] + [VMEM] * 2,
        out_specs=VMEM,
        compiler_params=params(),
        cost_estimate=cost(0.5),
        name="new_pair",
    )(place, own, y[0])
    bit = 1
    while bit < g2:
        g = plus(g, swap(g, bit, g1, False))
        g, new_pair = lax.optimization_barrier((g, new_pair))
        bit *= 2
    other = crop_swap(g, 1)
    first = place[1] == 0
    low, high = jnp.where(first, g, other), jnp.where(first, other, g)
    curvature = jnp.concatenate([p[n * chans : (n + 1) * chans].astype(F32) for p in (low, high) for n in range(3)], axis=1)
    return (new_pair[None], curvature)


def solution(mesh):
    placed = (P("crop", "axial", None, None), P("crop", None), P(), P())
    return jax.shard_map(
        shards,
        mesh=mesh,
        in_specs=placed,
        out_specs=(P("crop", "axial", None, None), P()),
        check_vma=False,
    )
```

```python
import functools

import jax
import jax.numpy as jnp
import numpy as np
from jax import lax
from jax.experimental import pallas as pl
from jax.experimental.pallas import tpu as pltpu
from jax.sharding import PartitionSpec as P

BF = jnp.bfloat16
F32 = jnp.float32
VMEM = pl.BlockSpec(memory_space=pltpu.VMEM)
ANY = pl.BlockSpec(memory_space=pl.ANY)
SMEM = pl.BlockSpec(memory_space=pltpu.SMEM)


def dot(left, right, dims=((1,), (0,))):
    return lax.dot_general(left, right, (dims, ((), ())), preferred_element_type=F32)


def log2(value):
    power = value.bit_length() - 1
    assert 1 << power == value
    return power


def centre(value):
    return value - jnp.mean(value, axis=1, keepdims=True)


def scale_of(centered):
    return lax.rsqrt(jnp.mean(centered * centered, axis=1, keepdims=True) + 1e-05)


def sigmoid(value):
    return 0.5 * jnp.tanh(0.5 * value) + 0.5


def flip(value, bits):
    return sum(((value >> b) & 1) << (bits - 1 - b) for b in range(bits))


def turned(core, value, bits):
    return jnp.where(core == 0, value, flip(value, bits))


def picker(cfg, place):
    g1, g2, rows, width, _, _ = cfg
    shape = (g2 * rows, width)
    spot = lax.broadcasted_iota(jnp.int32, shape, 0)
    col = lax.broadcasted_iota(jnp.int32, shape, 1)
    owner = jnp.bitwise_xor(place[0], turned(place[1], spot >> log2(rows), log2(g2)) * g1)
    return jnp.where(col == owner * rows + (spot & (rows - 1)), 1.0, 0.0).astype(BF)


def fill_side(cfg, place, mask_s, mask_v, w_ref, v_ref, blocks, step, first, outs):
    g1, g2, rows, width, chans, _ = cfg
    z_s, val_s, tan_s, sig_s, gate_s, *zp_s = outs
    if zp_s:
        pick = picker(cfg, place)
    blk = rows * width
    bits = log2(g1 if step == 1 else g2)
    for m, ref in blocks:
        here = slice(m * blk, (m + 1) * blk)
        value = centre(ref[...].reshape(blk, chans).astype(F32))
        zn = (value * scale_of(value)).astype(BF)
        z_s[:, here] = zn.T
        for r in range(rows if zp_s else 0):
            i = m * rows + r
            pairs = dot(pick, zn[r * width : (r + 1) * width]).astype(BF)
            zp_s[0][i * g2 * rows : (i + 1) * g2 * rows, :] = pairs
        proj = dot(zn, w_ref[:, first : first + 2 * chans])
        tang = dot(zn, v_ref[:, first : first + 2 * chans])
        base = jnp.bitwise_xor(place[0], turned(place[1], m, bits) * step) * rows
        cover = jnp.concatenate(
            [mask_v[...] * mask_s[0, base + r].astype(F32) for r in range(rows)], axis=0
        )
        sig = sigmoid(proj[:, chans:])
        held = cover * sig
        val = held * proj[:, :chans]
        gate = val - val * sig
        val_s[here, :] = val.astype(val_s.dtype)
        tan_s[here, :] = (held * tang[:, :chans] + gate * tang[:, chans:]).astype(tan_s.dtype)
        sig_s[here, :] = held.astype(sig_s.dtype)
        gate_s[here, :] = gate.astype(gate_s.dtype)


def own_kernel(cfg, place, mask_s, mask_v, w_ref, v_ref, own_ref, far_ref, *outs):
    g1, chans = cfg[0], cfg[4]
    fill_side(cfg, place, mask_s, mask_v, w_ref, v_ref, [(0, own_ref), (g1 - 1, far_ref)], 1, 0, outs[:6])
    fill_side(cfg, place, mask_s, mask_v, w_ref, v_ref, [(0, own_ref)], g1, 2 * chans, outs[6:])


def triangle(cfg, first, count, a_s, ta_s, b_s, tb_s, px_s, pt_s, x_ref, tx_ref):
    _, g2, rows, width, chans, _ = cfg
    n_j = g2 * rows

    def fold(value):
        return jnp.sum(value.reshape(width // 8, 8, chans), axis=0)

    def tri(i, carry):
        at = pl.ds(pl.multiple_of((first + i) * width, width), width)
        a, ta = a_s[at, :].astype(F32), ta_s[at, :].astype(F32)
        for j in range(n_j):
            here = slice(j * width, (j + 1) * width)
            b, tb = b_s[here, :].astype(F32), tb_s[here, :].astype(F32)
            to = pl.ds(pl.multiple_of(i * (n_j * 8), 8) + j * 8, 8)
            px_s[to, :] = fold(a * b)
            pt_s[to, :] = fold(ta * b + a * tb)
        return carry

    lax.fori_loop(0, count, tri, 0, unroll=4 if width <= 64 else 1)
    pairs = count * n_j
    here = slice(first * n_j, (first + count) * n_j)
    for part, out in ((px_s, x_ref), (pt_s, tx_ref)):
        total = sum(part[pl.ds(s, pairs, stride=8), :] for s in range(8))
        out[here, :] = total.astype(BF).astype(F32)


def line_kernel(cfg, place, mask_s, mask_v, w_ref, v_ref, a_s, ta_s, *rest):
    g1, g2, rows, width, chans, _ = cfg
    refs, (*outs, x_ref, tx_ref, px_s, pt_s) = rest[: g2 - 1], rest[g2 + 4 :]
    fill_side(cfg, place, mask_s, mask_v, w_ref, v_ref,
              [(m + 1, refs[m]) for m in range(g2 - 1)], g1, 2 * chans, outs)
    triangle(cfg, 0, rows, a_s, ta_s, outs[1], outs[2], px_s, pt_s, x_ref, tx_ref)


def block_kernel(cfg, place, mask_s, mask_v, w_ref, v_s, zj_s, b_s, tb_s, sb_s, gb_s, x_in, tx_in, *rest):
    g1, g2, rows, width, chans, total = cfg
    refs = rest[: g1 - 2]
    (keep_ref, send_ref, y_ref, zi_s, a_s, ta_s, sa_s, ga_s, zp_s,
     px_s, pt_s, x_s, tx_s, xb_s, d_s, g_s) = rest[g1 + 4 :]
    n_i, n_j = g1 * rows, g2 * rows
    blk = rows * width
    core = place[1]
    fill_side(cfg, place, mask_s, mask_v, w_ref, v_s,
              [(m, refs[m - 1]) for m in range(g1 - 2, 0, -1)], 1, 0, (zi_s, a_s, ta_s, sa_s, ga_s, zp_s))
    x_s[: rows * n_j, :] = x_in[...]
    tx_s[: rows * n_j, :] = tx_in[...]
    triangle(cfg, rows, n_i - rows, a_s, ta_s, b_s, tb_s, px_s, pt_s, x_s, tx_s)
    pairs = n_i * n_j

    w_gate, w_out = w_ref[:, 4 * chans : 5 * chans], w_ref[:, 5 * chans :]
    v_gate, v_out = v_s[:, 4 * chans : 5 * chans], v_s[:, 5 * chans :]
    step = min(pairs, 128)
    for at in range(0, pairs, step):
        here = slice(at, at + step)
        zp = zp_s[here, :]
        xc = centre(x_s[here, :])
        inv = scale_of(xc)
        xhat = xc * inv
        xn = xhat.astype(BF)
        tc = centre(tx_s[here, :])
        txn = (inv * (tc - xhat * jnp.mean(xhat * tc, axis=1, keepdims=True))).astype(BF)
        out = dot(xn, w_out)
        t_out = dot(txn, w_out) + dot(xn, v_out)
        sig = sigmoid(dot(zp, w_gate))
        slope = sig * (1.0 - sig) * out
        y_ref[here, :] = (sig * out).astype(BF)
        bar = (sig * t_out + slope * dot(zp, v_gate)) * (1.0 / total)
        d_out = (bar * sig).astype(BF)
        d_gate = (bar * slope).astype(BF)
        part_gate = dot(zp, d_gate, ((0,), (0,)))
        part_out = dot(xn, d_out, ((0,), (0,)))
        if at == 0:
            g_s[1, chans : 2 * chans, :] = part_gate
            g_s[1, 2 * chans :, :] = part_out
        else:
            g_s[1, chans : 2 * chans, :] += part_gate
            g_s[1, 2 * chans :, :] += part_out
        dxn = dot(d_out, w_out, ((1,), (1,)))
        dc = centre(dxn)
        xb_s[here, :] = inv * (dc - xhat * jnp.mean(xhat * dxn, axis=1, keepdims=True))

    chunk = min(width, 64)

    def back(count, others, row_of, val_s, sig_s, gate_s, z_s, spots):
        def one(m, carry):
            bars = [[] for _ in range(rows)]
            for kc in range(0, width, chunk):
                sums = [None] * rows
                for o in range(others):
                    val = val_s[o * width + kc : o * width + kc + chunk, :].astype(F32)
                    for r in range(rows):
                        term = xb_s[pl.ds(row_of(m * rows + r, o), 1), :] * val
                        sums[r] = term if o == 0 else sums[r] + term
                for r in range(rows):
                    bars[r].append(sums[r])
            bars = sum(bars, [])
            at = pl.ds(pl.multiple_of(m * blk, blk), blk)
            bar = jnp.concatenate(bars, axis=0)
            d_s[at, :chans] = (bar * sig_s[at, :].astype(F32)).astype(BF)
            d_s[at, chans:] = (bar * gate_s[at, :].astype(F32)).astype(BF)
            return carry

        lax.fori_loop(0, count, one, 0, unroll=width <= 64)
        part = dot(z_s[...], d_s[: count * blk, :])
        for n, (half, top) in enumerate(spots):
            g_s[half, top : top + chans, :] = part[:, n * chans : (n + 1) * chans]

    back(g1, n_j, lambda i, j: i * n_j + j, b_s, sa_s, ga_s, zi_s, ((0, 0), (0, chans)))
    back(g2, n_i, lambda j, i: i * n_j + j, a_s, sb_s, gb_s, zj_s, ((0, 2 * chans), (1, 0)))
    keep_ref[...] = g_s[core].astype(BF)
    send_ref[...] = g_s[1 - core].astype(BF)


def pair_kernel(cfg, place, pair_ref, y_ref, new_ref):
    g1, g2, rows, width, _, _ = cfg
    me, core = place[0], place[1]
    n_j = g2 * rows
    col = lax.broadcasted_iota(jnp.int32, (width, width), 0)
    spot = lax.broadcasted_iota(jnp.int32, (width, width), 1)
    n = turned(core, (spot >> log2(rows)) & (g2 - 1), log2(g2))
    s = turned(core, spot >> log2(n_j), log2(g1))
    owner = jnp.bitwise_xor(jnp.bitwise_xor(me, n * g1), s)
    put = jnp.where(col == owner * rows + (spot & (rows - 1)), 1.0, 0.0).astype(BF)
    for r in range(rows):
        y = jnp.concatenate([y_ref[s, r * n_j : (r + 1) * n_j, :] for s in range(g1)], axis=0)
        new_ref[r] = (pair_ref[r].astype(F32) + dot(put, y)).astype(BF)


def shards(pair, crop_mask, weights, probe_signs):
    own = pair[0]
    rows, width, chans = own.shape
    n_axial, n_crop = lax.axis_size("axial"), lax.axis_size("crop")
    g1 = 1 << (log2(n_axial) // 2)
    g2 = n_axial // g1
    n_i, n_j = g1 * rows, g2 * rows
    cfg = (g1, g2, rows, width, chans, n_crop * width * width)

    def crop_swap(value, bit):
        return lax.ppermute(value, "crop", [(i, i ^ bit) for i in range(n_crop)])

    def swap(value, m, step, mixed=True):
        bits = log2(g1 if step == 1 else g2)
        pairs = []
        for q in range(n_crop):
            there = (flip(m, bits) if mixed and q & 1 else m) * step
            pairs += [(q * n_axial + i, q * n_axial + (i ^ there)) for i in range(n_axial)]
        return lax.ppermute(value, ("crop", "axial"), pairs)

    along = [swap(own, m, g1) for m in range(1, g2)]
    place = jnp.stack([lax.axis_index("axial"), lax.axis_index("crop") & 1]).astype(jnp.int32)
    mask_v = jnp.broadcast_to(crop_mask[0].astype(F32)[:, None], (width, chans))
    kept = F32 if width <= 64 else BF
    shape = jax.ShapeDtypeStruct
    pairs = (n_i * n_j, chans)
    side = lambda n: [shape((chans, n * width), BF)] + [shape((n * width, chans), t) for t in (kept,) * 4]
    side_a, side_b = side(n_i) + [shape(pairs, BF)], side(n_j)
    half = shape((3 * chans, chans), BF)
    params = lambda: pltpu.CompilerParams(vmem_limit_bytes=(40 if width <= 64 else 58) << 20)
    cost = lambda us: pl.CostEstimate(flops=int(us * 1e9), bytes_accessed=0, transcendentals=0)

    unit = 1.0 / np.sqrt(np.float32(chans))
    v = ((2 * probe_signs - 1).astype(F32) * unit).astype(BF)
    later, v = lax.optimization_barrier((own, v))
    last, along[-1] = lax.optimization_barrier((later, along[-1]))
    starts = [last] + [later] * (g1 - 3) + [own]
    plane = [swap(starts[m - 1], m, 1) for m in range(1, g1)]
    sides = pl.pallas_call(
        functools.partial(own_kernel, cfg),
        out_shape=side_a + side_b,
        in_specs=[SMEM, SMEM] + [VMEM] * 5,
        out_specs=[VMEM] * 11,
        compiler_params=params(),
        cost_estimate=cost(0.01),
        name="own_rows",
    )(place, crop_mask, mask_v, weights, v, own, plane[-1])
    own_pairs = shape((rows * n_j, chans), F32)
    part = pltpu.VMEM((rows * n_j * 8, chans), F32)
    *line, x, tx = pl.pallas_call(
        functools.partial(line_kernel, cfg),
        out_shape=side_b + [own_pairs, own_pairs],
        in_specs=[SMEM, SMEM] + [VMEM] * (5 + g2 - 1 + 5),
        out_specs=[VMEM] * 7,
        input_output_aliases={6 + g2 + i: i for i in range(5)},
        scratch_shapes=[part, part],
        compiler_params=params(),
        cost_estimate=cost(0.01),
        name="line",
    )(place, crop_mask, mask_v, weights, v, sides[1], sides[2], *along, *sides[6:])
    part = pltpu.VMEM(((n_i - rows) * n_j * 8, chans), F32)
    keep, send, y, *_ = pl.pallas_call(
        functools.partial(block_kernel, cfg),
        out_shape=[half, half, shape(pairs, BF)] + side_a,
        in_specs=[SMEM, SMEM] + [VMEM] * (10 + g1 - 2 + 6),
        out_specs=[VMEM] * 9,
        input_output_aliases={10 + g1 + i: 3 + i for i in range(6)},
        scratch_shapes=[part, part]
        + [pltpu.VMEM(pairs, F32)] * 3
        + [pltpu.VMEM((max(n_i, n_j) * width, 2 * chans), BF)]
        + [pltpu.VMEM((2, 3 * chans, chans), F32)],
        compiler_params=params(),
        cost_estimate=cost(5.0),
        name="block",
    )(place, crop_mask, mask_v, weights, v, *line, x, tx, *plane[:-1], *sides[:6])

    def plus(one, two):
        return (one.astype(F32) + two.astype(F32)).astype(BF)

    g = plus(keep, crop_swap(send, 1))
    bit = 2
    while bit < n_crop:
        g = plus(g, crop_swap(g, bit))
        bit *= 2
    y = y.reshape(g1, 1, rows * n_j, chans)
    bit = 1
    while bit < g1:
        parts = y.reshape((y.shape[0] // 2, 2) + y.shape[1:])
        out = parts[:, 1].reshape(-1, chans)
        got = swap(jnp.concatenate([g, out], axis=0), bit, 1)
        g = plus(g, got[: 3 * chans])
        y = jnp.concatenate([parts[:, 0], got[3 * chans :].reshape(parts[:, 1].shape)], axis=1)
        bit *= 2
    new_pair = pl.pallas_call(
        functools.partial(pair_kernel, cfg),
        out_shape=shape(own.shape, BF),
        in_specs=[SMEM] + [VMEM] * 2,
        out_specs=VMEM,
        compiler_params=params(),
        cost_estimate=cost(0.5),
        name="new_pair",
    )(place, own, y[0])
    bit = 1
    while bit < g2:
        g = plus(g, swap(g, bit, g1, False))
        g, new_pair = lax.optimization_barrier((g, new_pair))
        bit *= 2
    other = crop_swap(g, 1)
    first = place[1] == 0
    low, high = jnp.where(first, g, other), jnp.where(first, other, g)
    curvature = jnp.concatenate([p[n * chans : (n + 1) * chans].astype(F32) for p in (low, high) for n in range(3)], axis=1)
    return (new_pair[None], curvature)


def solution(mesh):
    placed = (P("crop", "axial", None, None), P("crop", None), P(), P())
    return jax.shard_map(
        shards,
        mesh=mesh,
        in_specs=placed,
        out_specs=(P("crop", "axial", None, None), P()),
        check_vma=False,
    )
```

```python
import functools

import jax
import jax.numpy as jnp
import numpy as np
from jax import lax
from jax.experimental import pallas as pl
from jax.experimental.pallas import tpu as pltpu
from jax.sharding import PartitionSpec as P

BF = jnp.bfloat16
F32 = jnp.float32
VMEM = pl.BlockSpec(memory_space=pltpu.VMEM)
ANY = pl.BlockSpec(memory_space=pl.ANY)
SMEM = pl.BlockSpec(memory_space=pltpu.SMEM)


def dot(left, right, dims=((1,), (0,))):
    return lax.dot_general(left, right, (dims, ((), ())), preferred_element_type=F32)


def log2(value):
    power = value.bit_length() - 1
    assert 1 << power == value
    return power


def centre(value):
    return value - jnp.mean(value, axis=1, keepdims=True)


def scale_of(centered):
    return lax.rsqrt(jnp.mean(centered * centered, axis=1, keepdims=True) + 1e-05)


def sigmoid(value):
    return 0.5 * jnp.tanh(0.5 * value) + 0.5


def flip(value, bits):
    return sum(((value >> b) & 1) << (bits - 1 - b) for b in range(bits))


def turned(core, value, bits):
    return jnp.where(core == 0, value, flip(value, bits))


def picker(cfg, place):
    g1, g2, rows, width, _, _ = cfg
    shape = (g2 * rows, width)
    spot = lax.broadcasted_iota(jnp.int32, shape, 0)
    col = lax.broadcasted_iota(jnp.int32, shape, 1)
    owner = jnp.bitwise_xor(place[0], turned(place[1], spot >> log2(rows), log2(g2)) * g1)
    return jnp.where(col == owner * rows + (spot & (rows - 1)), 1.0, 0.0).astype(BF)


def fill_side(cfg, place, mask_s, mask_v, w_ref, v_ref, blocks, step, first, outs):
    g1, g2, rows, width, chans, _ = cfg
    z_s, val_s, tan_s, sig_s, gate_s, *zp_s = outs
    if zp_s:
        pick = picker(cfg, place)
    blk = rows * width
    bits = log2(g1 if step == 1 else g2)
    for m, ref in blocks:
        here = slice(m * blk, (m + 1) * blk)
        value = centre(ref[...].reshape(blk, chans).astype(F32))
        zn = (value * scale_of(value)).astype(BF)
        z_s[:, here] = zn.T
        for r in range(rows if zp_s else 0):
            i = m * rows + r
            pairs = dot(pick, zn[r * width : (r + 1) * width]).astype(BF)
            zp_s[0][i * g2 * rows : (i + 1) * g2 * rows, :] = pairs
        proj = dot(zn, w_ref[:, first : first + 2 * chans])
        tang = dot(zn, v_ref[:, first : first + 2 * chans])
        base = jnp.bitwise_xor(place[0], turned(place[1], m, bits) * step) * rows
        cover = jnp.concatenate(
            [mask_v[...] * mask_s[0, base + r].astype(F32) for r in range(rows)], axis=0
        )
        sig = sigmoid(proj[:, chans:])
        held = cover * sig
        val = held * proj[:, :chans]
        gate = val - val * sig
        val_s[here, :] = val.astype(val_s.dtype)
        tan_s[here, :] = (held * tang[:, :chans] + gate * tang[:, chans:]).astype(tan_s.dtype)
        sig_s[here, :] = held.astype(sig_s.dtype)
        gate_s[here, :] = gate.astype(gate_s.dtype)


def own_kernel(cfg, place, mask_s, mask_v, w_ref, v_ref, own_ref, far_ref, *outs):
    g1, chans = cfg[0], cfg[4]
    fill_side(cfg, place, mask_s, mask_v, w_ref, v_ref, [(0, own_ref), (g1 - 1, far_ref)], 1, 0, outs[:6])
    fill_side(cfg, place, mask_s, mask_v, w_ref, v_ref, [(0, own_ref)], g1, 2 * chans, outs[6:])


def triangle(cfg, first, count, a_s, ta_s, b_s, tb_s, px_s, pt_s, x_ref, tx_ref):
    _, g2, rows, width, chans, _ = cfg
    n_j = g2 * rows

    def fold(value):
        return jnp.sum(value.reshape(width // 8, 8, chans), axis=0)

    def tri(i, carry):
        at = pl.ds(pl.multiple_of((first + i) * width, width), width)
        a, ta = a_s[at, :].astype(F32), ta_s[at, :].astype(F32)
        for j in range(n_j):
            here = slice(j * width, (j + 1) * width)
            b, tb = b_s[here, :].astype(F32), tb_s[here, :].astype(F32)
            to = pl.ds(pl.multiple_of(i * (n_j * 8), 8) + j * 8, 8)
            px_s[to, :] = fold(a * b)
            pt_s[to, :] = fold(ta * b + a * tb)
        return carry

    lax.fori_loop(0, count, tri, 0, unroll=4 if width <= 64 else 1)
    pairs = count * n_j
    here = slice(first * n_j, (first + count) * n_j)
    for part, out in ((px_s, x_ref), (pt_s, tx_ref)):
        total = sum(part[pl.ds(s, pairs, stride=8), :] for s in range(8))
        out[here, :] = total.astype(BF).astype(F32)


def line_kernel(cfg, place, mask_s, mask_v, w_ref, v_ref, a_s, ta_s, *rest):
    g1, g2, rows, width, chans, _ = cfg
    refs, (*outs, x_ref, tx_ref, px_s, pt_s) = rest[: g2 - 1], rest[g2 + 4 :]
    fill_side(cfg, place, mask_s, mask_v, w_ref, v_ref,
              [(m + 1, refs[m]) for m in range(g2 - 1)], g1, 2 * chans, outs)
    triangle(cfg, 0, rows, a_s, ta_s, outs[1], outs[2], px_s, pt_s, x_ref, tx_ref)


def block_kernel(cfg, place, mask_s, mask_v, w_ref, v_s, zj_s, b_s, tb_s, sb_s, gb_s, x_in, tx_in, *rest):
    g1, g2, rows, width, chans, total = cfg
    refs = rest[: g1 - 2]
    (keep_ref, send_ref, y_ref, zi_s, a_s, ta_s, sa_s, ga_s, zp_s,
     px_s, pt_s, x_s, tx_s, xb_s, d_s, g_s) = rest[g1 + 4 :]
    n_i, n_j = g1 * rows, g2 * rows
    blk = rows * width
    core = place[1]
    fill_side(cfg, place, mask_s, mask_v, w_ref, v_s,
              [(m, refs[m - 1]) for m in range(g1 - 2, 0, -1)], 1, 0, (zi_s, a_s, ta_s, sa_s, ga_s, zp_s))
    x_s[: rows * n_j, :] = x_in[...]
    tx_s[: rows * n_j, :] = tx_in[...]
    triangle(cfg, rows, n_i - rows, a_s, ta_s, b_s, tb_s, px_s, pt_s, x_s, tx_s)
    pairs = n_i * n_j

    w_gate, w_out = w_ref[:, 4 * chans : 5 * chans], w_ref[:, 5 * chans :]
    v_gate, v_out = v_s[:, 4 * chans : 5 * chans], v_s[:, 5 * chans :]
    step = min(pairs, 128)
    for at in range(0, pairs, step):
        here = slice(at, at + step)
        zp = zp_s[here, :]
        xc = centre(x_s[here, :])
        inv = scale_of(xc)
        xhat = xc * inv
        xn = xhat.astype(BF)
        tc = centre(tx_s[here, :])
        txn = (inv * (tc - xhat * jnp.mean(xhat * tc, axis=1, keepdims=True))).astype(BF)
        out = dot(xn, w_out)
        t_out = dot(txn, w_out) + dot(xn, v_out)
        sig = sigmoid(dot(zp, w_gate))
        slope = sig * (1.0 - sig) * out
        y_ref[here, :] = (sig * out).astype(BF)
        bar = (sig * t_out + slope * dot(zp, v_gate)) * (1.0 / total)
        d_out = (bar * sig).astype(BF)
        d_gate = (bar * slope).astype(BF)
        part_gate = dot(zp, d_gate, ((0,), (0,)))
        part_out = dot(xn, d_out, ((0,), (0,)))
        if at == 0:
            g_s[1, chans : 2 * chans, :] = part_gate
            g_s[1, 2 * chans :, :] = part_out
        else:
            g_s[1, chans : 2 * chans, :] += part_gate
            g_s[1, 2 * chans :, :] += part_out
        dxn = dot(d_out, w_out, ((1,), (1,)))
        dc = centre(dxn)
        xb_s[here, :] = inv * (dc - xhat * jnp.mean(xhat * dxn, axis=1, keepdims=True))

    chunk = min(width, 64)

    def back(count, others, row_of, val_s, sig_s, gate_s, z_s, spots):
        def one(m, carry):
            bars = [[] for _ in range(rows)]
            for kc in range(0, width, chunk):
                sums = [None] * rows
                for o in range(others):
                    val = val_s[o * width + kc : o * width + kc + chunk, :].astype(F32)
                    for r in range(rows):
                        term = xb_s[pl.ds(row_of(m * rows + r, o), 1), :] * val
                        sums[r] = term if o == 0 else sums[r] + term
                for r in range(rows):
                    bars[r].append(sums[r])
            bars = sum(bars, [])
            at = pl.ds(pl.multiple_of(m * blk, blk), blk)
            bar = jnp.concatenate(bars, axis=0)
            d_s[at, :chans] = (bar * sig_s[at, :].astype(F32)).astype(BF)
            d_s[at, chans:] = (bar * gate_s[at, :].astype(F32)).astype(BF)
            return carry

        lax.fori_loop(0, count, one, 0, unroll=width <= 64)
        part = dot(z_s[...], d_s[: count * blk, :])
        for n, (half, top) in enumerate(spots):
            g_s[half, top : top + chans, :] = part[:, n * chans : (n + 1) * chans]

    back(g1, n_j, lambda i, j: i * n_j + j, b_s, sa_s, ga_s, zi_s, ((0, 0), (0, chans)))
    back(g2, n_i, lambda j, i: i * n_j + j, a_s, sb_s, gb_s, zj_s, ((0, 2 * chans), (1, 0)))
    keep_ref[...] = g_s[core].astype(BF)
    send_ref[...] = g_s[1 - core].astype(BF)


def pair_kernel(cfg, place, pair_ref, y_ref, new_ref):
    g1, g2, rows, width, _, _ = cfg
    me, core = place[0], place[1]
    n_j = g2 * rows
    col = lax.broadcasted_iota(jnp.int32, (width, width), 0)
    spot = lax.broadcasted_iota(jnp.int32, (width, width), 1)
    n = turned(core, (spot >> log2(rows)) & (g2 - 1), log2(g2))
    s = turned(core, spot >> log2(n_j), log2(g1))
    owner = jnp.bitwise_xor(jnp.bitwise_xor(me, n * g1), s)
    put = jnp.where(col == owner * rows + (spot & (rows - 1)), 1.0, 0.0).astype(BF)
    for r in range(rows):
        y = jnp.concatenate([y_ref[s, r * n_j : (r + 1) * n_j, :] for s in range(g1)], axis=0)
        new_ref[r] = (pair_ref[r].astype(F32) + dot(put, y)).astype(BF)


def shards(pair, crop_mask, weights, probe_signs):
    own = pair[0]
    rows, width, chans = own.shape
    n_axial, n_crop = lax.axis_size("axial"), lax.axis_size("crop")
    g1 = 1 << (log2(n_axial) // 2)
    g2 = n_axial // g1
    n_i, n_j = g1 * rows, g2 * rows
    cfg = (g1, g2, rows, width, chans, n_crop * width * width)

    def crop_swap(value, bit):
        return lax.ppermute(value, "crop", [(i, i ^ bit) for i in range(n_crop)])

    def swap(value, m, step, mixed=True):
        bits = log2(g1 if step == 1 else g2)
        pairs = []
        for q in range(n_crop):
            there = (flip(m, bits) if mixed and q & 1 else m) * step
            pairs += [(q * n_axial + i, q * n_axial + (i ^ there)) for i in range(n_axial)]
        return lax.ppermute(value, ("crop", "axial"), pairs)

    along = [swap(own, m, g1) for m in range(1, g2)]
    place = jnp.stack([lax.axis_index("axial"), lax.axis_index("crop") & 1]).astype(jnp.int32)
    mask_v = jnp.broadcast_to(crop_mask[0].astype(F32)[:, None], (width, chans))
    kept = F32 if width <= 64 else BF
    shape = jax.ShapeDtypeStruct
    pairs = (n_i * n_j, chans)
    side = lambda n: [shape((chans, n * width), BF)] + [shape((n * width, chans), t) for t in (kept,) * 4]
    side_a, side_b = side(n_i) + [shape(pairs, BF)], side(n_j)
    half = shape((3 * chans, chans), BF)
    params = lambda: pltpu.CompilerParams(vmem_limit_bytes=(40 if width <= 64 else 58) << 20)
    cost = lambda us: pl.CostEstimate(flops=int(us * 1e9), bytes_accessed=0, transcendentals=0)

    unit = 1.0 / np.sqrt(np.float32(chans))
    v = ((2 * probe_signs - 1).astype(F32) * unit).astype(BF)
    later, v = lax.optimization_barrier((own, v))
    last, along[-1] = lax.optimization_barrier((later, along[-1]))
    starts = [last] + [later] * (g1 - 3) + [own]
    plane = [swap(starts[m - 1], m, 1) for m in range(1, g1)]
    sides = pl.pallas_call(
        functools.partial(own_kernel, cfg),
        out_shape=side_a + side_b,
        in_specs=[SMEM, SMEM] + [VMEM] * 5,
        out_specs=[VMEM] * 11,
        compiler_params=params(),
        cost_estimate=cost(0.01),
        name="own_rows",
    )(place, crop_mask, mask_v, weights, v, own, plane[-1])
    own_pairs = shape((rows * n_j, chans), F32)
    part = pltpu.VMEM((rows * n_j * 8 + 8, chans), F32)
    *line, x, tx = pl.pallas_call(
        functools.partial(line_kernel, cfg),
        out_shape=side_b + [own_pairs, own_pairs],
        in_specs=[SMEM, SMEM] + [VMEM] * (5 + g2 - 1 + 5),
        out_specs=[VMEM] * 7,
        input_output_aliases={6 + g2 + i: i for i in range(5)},
        scratch_shapes=[part, part],
        compiler_params=params(),
        cost_estimate=cost(0.01),
        name="line",
    )(place, crop_mask, mask_v, weights, v, sides[1], sides[2], *along, *sides[6:])
    part = pltpu.VMEM(((n_i - rows) * n_j * 8 + 8, chans), F32)
    keep, send, y, *_ = pl.pallas_call(
        functools.partial(block_kernel, cfg),
        out_shape=[half, half, shape(pairs, BF)] + side_a,
        in_specs=[SMEM, SMEM] + [VMEM] * (10 + g1 - 2 + 6),
        out_specs=[VMEM] * 9,
        input_output_aliases={10 + g1 + i: 3 + i for i in range(6)},
        scratch_shapes=[part, part]
        + [pltpu.VMEM(pairs, F32)] * 3
        + [pltpu.VMEM((max(n_i, n_j) * width, 2 * chans), BF)]
        + [pltpu.VMEM((2, 3 * chans, chans), F32)],
        compiler_params=params(),
        cost_estimate=cost(5.0),
        name="block",
    )(place, crop_mask, mask_v, weights, v, *line, x, tx, *plane[:-1], *sides[:6])

    def plus(one, two):
        return (one.astype(F32) + two.astype(F32)).astype(BF)

    g = plus(keep, crop_swap(send, 1))
    bit = 2
    while bit < n_crop:
        g = plus(g, crop_swap(g, bit))
        bit *= 2
    y = y.reshape(g1, 1, rows * n_j, chans)
    bit = 1
    while bit < g1:
        parts = y.reshape((y.shape[0] // 2, 2) + y.shape[1:])
        out = parts[:, 1].reshape(-1, chans)
        got = swap(jnp.concatenate([g, out], axis=0), bit, 1)
        g = plus(g, got[: 3 * chans])
        y = jnp.concatenate([parts[:, 0], got[3 * chans :].reshape(parts[:, 1].shape)], axis=1)
        bit *= 2
    new_pair = pl.pallas_call(
        functools.partial(pair_kernel, cfg),
        out_shape=shape(own.shape, BF),
        in_specs=[SMEM] + [VMEM] * 2,
        out_specs=VMEM,
        compiler_params=params(),
        cost_estimate=cost(0.5),
        name="new_pair",
    )(place, own, y[0])
    bit = 1
    while bit < g2:
        g = plus(g, swap(g, bit, g1, False))
        g, new_pair = lax.optimization_barrier((g, new_pair))
        bit *= 2
    other = crop_swap(g, 1)
    first = place[1] == 0
    low, high = jnp.where(first, g, other), jnp.where(first, other, g)
    curvature = jnp.concatenate([p[n * chans : (n + 1) * chans].astype(F32) for p in (low, high) for n in range(3)], axis=1)
    return (new_pair[None], curvature)


def solution(mesh):
    placed = (P("crop", "axial", None, None), P("crop", None), P(), P())
    return jax.shard_map(
        shards,
        mesh=mesh,
        in_specs=placed,
        out_specs=(P("crop", "axial", None, None), P()),
        check_vma=False,
    )
```

```python
import functools

import jax
import jax.numpy as jnp
import numpy as np
from jax import lax
from jax.experimental import pallas as pl
from jax.experimental.pallas import tpu as pltpu
from jax.sharding import PartitionSpec as P

BF = jnp.bfloat16
F32 = jnp.float32
VMEM = pl.BlockSpec(memory_space=pltpu.VMEM)
ANY = pl.BlockSpec(memory_space=pl.ANY)
SMEM = pl.BlockSpec(memory_space=pltpu.SMEM)


def dot(left, right, dims=((1,), (0,))):
    return lax.dot_general(left, right, (dims, ((), ())), preferred_element_type=F32)


def log2(value):
    power = value.bit_length() - 1
    assert 1 << power == value
    return power


def centre(value):
    return value - jnp.mean(value, axis=1, keepdims=True)


def scale_of(centered):
    return lax.rsqrt(jnp.mean(centered * centered, axis=1, keepdims=True) + 1e-05)


def sigmoid(value):
    return 0.5 * jnp.tanh(0.5 * value) + 0.5


def flip(value, bits):
    return sum(((value >> b) & 1) << (bits - 1 - b) for b in range(bits))


def turned(core, value, bits):
    return jnp.where(core == 0, value, flip(value, bits))


def picker(cfg, place):
    g1, g2, rows, width, _, _ = cfg
    shape = (g2 * rows, width)
    spot = lax.broadcasted_iota(jnp.int32, shape, 0)
    col = lax.broadcasted_iota(jnp.int32, shape, 1)
    owner = jnp.bitwise_xor(place[0], turned(place[1], spot >> log2(rows), log2(g2)) * g1)
    return jnp.where(col == owner * rows + (spot & (rows - 1)), 1.0, 0.0).astype(BF)


def fill_side(cfg, place, mask_s, mask_v, w_ref, v_ref, blocks, step, first, outs):
    g1, g2, rows, width, chans, _ = cfg
    z_s, val_s, tan_s, sig_s, gate_s, *zp_s = outs
    if zp_s:
        pick = picker(cfg, place)
    blk = rows * width
    bits = log2(g1 if step == 1 else g2)
    for m, ref in blocks:
        here = slice(m * blk, (m + 1) * blk)
        value = centre(ref[...].reshape(blk, chans).astype(F32))
        zn = (value * scale_of(value)).astype(BF)
        z_s[:, here] = zn.T
        for r in range(rows if zp_s else 0):
            i = m * rows + r
            pairs = dot(pick, zn[r * width : (r + 1) * width]).astype(BF)
            zp_s[0][i * g2 * rows : (i + 1) * g2 * rows, :] = pairs
        proj = dot(zn, w_ref[:, first : first + 2 * chans])
        tang = dot(zn, v_ref[:, first : first + 2 * chans])
        base = jnp.bitwise_xor(place[0], turned(place[1], m, bits) * step) * rows
        cover = jnp.concatenate(
            [mask_v[...] * mask_s[0, base + r].astype(F32) for r in range(rows)], axis=0
        )
        sig = sigmoid(proj[:, chans:])
        held = cover * sig
        val = held * proj[:, :chans]
        gate = val - val * sig
        val_s[here, :] = val.astype(val_s.dtype)
        tan_s[here, :] = (held * tang[:, :chans] + gate * tang[:, chans:]).astype(tan_s.dtype)
        sig_s[here, :] = held.astype(sig_s.dtype)
        gate_s[here, :] = gate.astype(gate_s.dtype)


def own_kernel(cfg, place, mask_s, mask_v, w_ref, v_ref, own_ref, *outs):
    g1, chans = cfg[0], cfg[4]
    fill_side(cfg, place, mask_s, mask_v, w_ref, v_ref, [(0, own_ref)], 1, 0, outs[:6])
    fill_side(cfg, place, mask_s, mask_v, w_ref, v_ref, [(0, own_ref)], g1, 2 * chans, outs[6:])


def triangle(cfg, first, count, a_s, ta_s, b_s, tb_s, px_s, pt_s, x_ref, tx_ref):
    _, g2, rows, width, chans, _ = cfg
    n_j = g2 * rows

    def fold(value):
        return jnp.sum(value.reshape(width // 8, 8, chans), axis=0)

    def tri(i, carry):
        at = pl.ds(pl.multiple_of((first + i) * width, width), width)
        a, ta = a_s[at, :].astype(F32), ta_s[at, :].astype(F32)
        for j in range(n_j):
            here = slice(j * width, (j + 1) * width)
            b, tb = b_s[here, :].astype(F32), tb_s[here, :].astype(F32)
            to = pl.ds(pl.multiple_of(i * (n_j * 8), 8) + j * 8, 8)
            px_s[to, :] = fold(a * b)
            pt_s[to, :] = fold(ta * b + a * tb)
        return carry

    lax.fori_loop(0, count, tri, 0, unroll=4 if width <= 64 else 1)
    pairs = count * n_j
    here = slice(first * n_j, (first + count) * n_j)
    for part, out in ((px_s, x_ref), (pt_s, tx_ref)):
        total = sum(part[pl.ds(s, pairs, stride=8), :] for s in range(8))
        out[here, :] = total.astype(BF).astype(F32)


def line_kernel(cfg, place, mask_s, mask_v, w_ref, v_ref, *rest):
    g1, g2, rows, width, chans, _ = cfg
    refs, (*outs, x_ref, tx_ref, px_s, pt_s) = rest[:g2], rest[g2 + 11 :]
    fill_side(cfg, place, mask_s, mask_v, w_ref, v_ref,
              [(m + 1, refs[m]) for m in range(g2 - 1)], g1, 2 * chans, outs[6:])
    triangle(cfg, 0, rows, outs[1], outs[2], outs[7], outs[8], px_s, pt_s, x_ref, tx_ref)
    fill_side(cfg, place, mask_s, mask_v, w_ref, v_ref, [(g1 - 1, refs[g2 - 1])], 1, 0, outs[:6])


def block_kernel(cfg, place, mask_s, mask_v, w_ref, v_s, zj_s, b_s, tb_s, sb_s, gb_s, x_in, tx_in, *rest):
    g1, g2, rows, width, chans, total = cfg
    refs = rest[: g1 - 2]
    (keep_ref, send_ref, y_ref, zi_s, a_s, ta_s, sa_s, ga_s, zp_s,
     px_s, pt_s, x_s, tx_s, xb_s, d_s, g_s) = rest[g1 + 4 :]
    n_i, n_j = g1 * rows, g2 * rows
    blk = rows * width
    core = place[1]
    fill_side(cfg, place, mask_s, mask_v, w_ref, v_s,
              [(m, refs[m - 1]) for m in range(g1 - 2, 0, -1)], 1, 0, (zi_s, a_s, ta_s, sa_s, ga_s, zp_s))
    x_s[: rows * n_j, :] = x_in[...]
    tx_s[: rows * n_j, :] = tx_in[...]
    triangle(cfg, rows, n_i - rows, a_s, ta_s, b_s, tb_s, px_s, pt_s, x_s, tx_s)
    pairs = n_i * n_j

    w_gate, w_out = w_ref[:, 4 * chans : 5 * chans], w_ref[:, 5 * chans :]
    v_gate, v_out = v_s[:, 4 * chans : 5 * chans], v_s[:, 5 * chans :]
    step = min(pairs, 128)
    for at in range(0, pairs, step):
        here = slice(at, at + step)
        zp = zp_s[here, :]
        xc = centre(x_s[here, :])
        inv = scale_of(xc)
        xhat = xc * inv
        xn = xhat.astype(BF)
        tc = centre(tx_s[here, :])
        txn = (inv * (tc - xhat * jnp.mean(xhat * tc, axis=1, keepdims=True))).astype(BF)
        out = dot(xn, w_out)
        t_out = dot(txn, w_out) + dot(xn, v_out)
        sig = sigmoid(dot(zp, w_gate))
        slope = sig * (1.0 - sig) * out
        y_ref[here, :] = (sig * out).astype(BF)
        bar = (sig * t_out + slope * dot(zp, v_gate)) * (1.0 / total)
        d_out = (bar * sig).astype(BF)
        d_gate = (bar * slope).astype(BF)
        part_gate = dot(zp, d_gate, ((0,), (0,)))
        part_out = dot(xn, d_out, ((0,), (0,)))
        if at == 0:
            g_s[1, chans : 2 * chans, :] = part_gate
            g_s[1, 2 * chans :, :] = part_out
        else:
            g_s[1, chans : 2 * chans, :] += part_gate
            g_s[1, 2 * chans :, :] += part_out
        dxn = dot(d_out, w_out, ((1,), (1,)))
        dc = centre(dxn)
        xb_s[here, :] = inv * (dc - xhat * jnp.mean(xhat * dxn, axis=1, keepdims=True))

    chunk = min(width, 64)

    def back(count, others, row_of, val_s, sig_s, gate_s, z_s, spots):
        def one(m, carry):
            bars = [[] for _ in range(rows)]
            for kc in range(0, width, chunk):
                sums = [None] * rows
                for o in range(others):
                    val = val_s[o * width + kc : o * width + kc + chunk, :].astype(F32)
                    for r in range(rows):
                        term = xb_s[pl.ds(row_of(m * rows + r, o), 1), :] * val
                        sums[r] = term if o == 0 else sums[r] + term
                for r in range(rows):
                    bars[r].append(sums[r])
            bars = sum(bars, [])
            at = pl.ds(pl.multiple_of(m * blk, blk), blk)
            bar = jnp.concatenate(bars, axis=0)
            d_s[at, :chans] = (bar * sig_s[at, :].astype(F32)).astype(BF)
            d_s[at, chans:] = (bar * gate_s[at, :].astype(F32)).astype(BF)
            return carry

        lax.fori_loop(0, count, one, 0, unroll=width <= 64)
        part = dot(z_s[...], d_s[: count * blk, :])
        for n, (half, top) in enumerate(spots):
            g_s[half, top : top + chans, :] = part[:, n * chans : (n + 1) * chans]

    back(g1, n_j, lambda i, j: i * n_j + j, b_s, sa_s, ga_s, zi_s, ((0, 0), (0, chans)))
    back(g2, n_i, lambda j, i: i * n_j + j, a_s, sb_s, gb_s, zj_s, ((0, 2 * chans), (1, 0)))
    keep_ref[...] = g_s[core].astype(BF)
    send_ref[...] = g_s[1 - core].astype(BF)


def pair_kernel(cfg, place, pair_ref, y_ref, new_ref):
    g1, g2, rows, width, _, _ = cfg
    me, core = place[0], place[1]
    n_j = g2 * rows
    col = lax.broadcasted_iota(jnp.int32, (width, width), 0)
    spot = lax.broadcasted_iota(jnp.int32, (width, width), 1)
    n = turned(core, (spot >> log2(rows)) & (g2 - 1), log2(g2))
    s = turned(core, spot >> log2(n_j), log2(g1))
    owner = jnp.bitwise_xor(jnp.bitwise_xor(me, n * g1), s)
    put = jnp.where(col == owner * rows + (spot & (rows - 1)), 1.0, 0.0).astype(BF)
    for r in range(rows):
        y = jnp.concatenate([y_ref[s, r * n_j : (r + 1) * n_j, :] for s in range(g1)], axis=0)
        new_ref[r] = (pair_ref[r].astype(F32) + dot(put, y)).astype(BF)


def shards(pair, crop_mask, weights, probe_signs):
    own = pair[0]
    rows, width, chans = own.shape
    n_axial, n_crop = lax.axis_size("axial"), lax.axis_size("crop")
    g1 = 1 << (log2(n_axial) // 2)
    g2 = n_axial // g1
    n_i, n_j = g1 * rows, g2 * rows
    cfg = (g1, g2, rows, width, chans, n_crop * width * width)

    def crop_swap(value, bit):
        return lax.ppermute(value, "crop", [(i, i ^ bit) for i in range(n_crop)])

    def swap(value, m, step, mixed=True):
        bits = log2(g1 if step == 1 else g2)
        pairs = []
        for q in range(n_crop):
            there = (flip(m, bits) if mixed and q & 1 else m) * step
            pairs += [(q * n_axial + i, q * n_axial + (i ^ there)) for i in range(n_axial)]
        return lax.ppermute(value, ("crop", "axial"), pairs)

    along = [swap(own, m, g1) for m in range(1, g2)]
    place = jnp.stack([lax.axis_index("axial"), lax.axis_index("crop") & 1]).astype(jnp.int32)
    mask_v = jnp.broadcast_to(crop_mask[0].astype(F32)[:, None], (width, chans))
    kept = F32 if width <= 64 else BF
    shape = jax.ShapeDtypeStruct
    pairs = (n_i * n_j, chans)
    side = lambda n: [shape((chans, n * width), BF)] + [shape((n * width, chans), t) for t in (kept,) * 4]
    side_a, side_b = side(n_i) + [shape(pairs, BF)], side(n_j)
    half = shape((3 * chans, chans), BF)
    params = lambda: pltpu.CompilerParams(vmem_limit_bytes=(40 if width <= 64 else 58) << 20)
    cost = lambda us: pl.CostEstimate(flops=int(us * 1e9), bytes_accessed=0, transcendentals=0)

    unit = 1.0 / np.sqrt(np.float32(chans))
    v = ((2 * probe_signs - 1).astype(F32) * unit).astype(BF)
    later, v = lax.optimization_barrier((own, v))
    last, along[-1] = lax.optimization_barrier((later, along[-1]))
    starts = [last] + [later] * (g1 - 3) + [own]
    plane = [swap(starts[m - 1], m, 1) for m in range(1, g1)]
    sides = pl.pallas_call(
        functools.partial(own_kernel, cfg),
        out_shape=side_a + side_b,
        in_specs=[SMEM, SMEM] + [VMEM] * 4,
        out_specs=[VMEM] * 11,
        compiler_params=params(),
        cost_estimate=cost(0.01),
        name="own_rows",
    )(place, crop_mask, mask_v, weights, v, own)
    own_pairs = shape((rows * n_j, chans), F32)
    part = pltpu.VMEM((rows * n_j * 8 + 8, chans), F32)
    *sides, x, tx = pl.pallas_call(
        functools.partial(line_kernel, cfg),
        out_shape=side_a + side_b + [own_pairs, own_pairs],
        in_specs=[SMEM, SMEM] + [VMEM] * (3 + g2 + 11),
        out_specs=[VMEM] * 13,
        input_output_aliases={5 + g2 + i: i for i in range(11)},
        scratch_shapes=[part, part],
        compiler_params=params(),
        cost_estimate=cost(0.01),
        name="line",
    )(place, crop_mask, mask_v, weights, v, *along, plane[-1], *sides)
    part = pltpu.VMEM(((n_i - rows) * n_j * 8 + 8, chans), F32)
    keep, send, y, *_ = pl.pallas_call(
        functools.partial(block_kernel, cfg),
        out_shape=[half, half, shape(pairs, BF)] + side_a,
        in_specs=[SMEM, SMEM] + [VMEM] * (10 + g1 - 2 + 6),
        out_specs=[VMEM] * 9,
        input_output_aliases={10 + g1 + i: 3 + i for i in range(6)},
        scratch_shapes=[part, part]
        + [pltpu.VMEM(pairs, F32)] * 3
        + [pltpu.VMEM((max(n_i, n_j) * width, 2 * chans), BF)]
        + [pltpu.VMEM((2, 3 * chans, chans), F32)],
        compiler_params=params(),
        cost_estimate=cost(5.0),
        name="block",
    )(place, crop_mask, mask_v, weights, v, *sides[6:], x, tx, *plane[:-1], *sides[:6])

    def plus(one, two):
        return (one.astype(F32) + two.astype(F32)).astype(BF)

    g = plus(keep, crop_swap(send, 1))
    bit = 2
    while bit < n_crop:
        g = plus(g, crop_swap(g, bit))
        bit *= 2
    y = y.reshape(g1, 1, rows * n_j, chans)
    bit = 1
    while bit < g1:
        parts = y.reshape((y.shape[0] // 2, 2) + y.shape[1:])
        out = parts[:, 1].reshape(-1, chans)
        got = swap(jnp.concatenate([g, out], axis=0), bit, 1)
        g = plus(g, got[: 3 * chans])
        y = jnp.concatenate([parts[:, 0], got[3 * chans :].reshape(parts[:, 1].shape)], axis=1)
        bit *= 2
    new_pair = pl.pallas_call(
        functools.partial(pair_kernel, cfg),
        out_shape=shape(own.shape, BF),
        in_specs=[SMEM] + [VMEM] * 2,
        out_specs=VMEM,
        compiler_params=params(),
        cost_estimate=cost(0.5),
        name="new_pair",
    )(place, own, y[0])
    bit = 1
    while bit < g2:
        g = plus(g, swap(g, bit, g1))
        g, new_pair = lax.optimization_barrier((g, new_pair))
        bit *= 2
    other = crop_swap(g, 1)
    first = place[1] == 0
    low, high = jnp.where(first, g, other), jnp.where(first, other, g)
    curvature = jnp.concatenate([p[n * chans : (n + 1) * chans].astype(F32) for p in (low, high) for n in range(3)], axis=1)
    return (new_pair[None], curvature)


def solution(mesh):
    placed = (P("crop", "axial", None, None), P("crop", None), P(), P())
    return jax.shard_map(
        shards,
        mesh=mesh,
        in_specs=placed,
        out_specs=(P("crop", "axial", None, None), P()),
        check_vma=False,
    )
```

```python
import functools

import jax
import jax.numpy as jnp
import numpy as np
from jax import lax
from jax.experimental import pallas as pl
from jax.experimental.pallas import tpu as pltpu
from jax.sharding import PartitionSpec as P

BF = jnp.bfloat16
F32 = jnp.float32
VMEM = pl.BlockSpec(memory_space=pltpu.VMEM)
ANY = pl.BlockSpec(memory_space=pl.ANY)
SMEM = pl.BlockSpec(memory_space=pltpu.SMEM)


def dot(left, right, dims=((1,), (0,))):
    return lax.dot_general(left, right, (dims, ((), ())), preferred_element_type=F32)


def log2(value):
    power = value.bit_length() - 1
    assert 1 << power == value
    return power


def centre(value):
    return value - jnp.mean(value, axis=1, keepdims=True)


def scale_of(centered):
    return lax.rsqrt(jnp.mean(centered * centered, axis=1, keepdims=True) + 1e-05)


def sigmoid(value):
    return 0.5 * jnp.tanh(0.5 * value) + 0.5


def flip(value, bits):
    return sum(((value >> b) & 1) << (bits - 1 - b) for b in range(bits))


def turned(core, value, bits):
    return jnp.where(core == 0, value, flip(value, bits))


def picker(cfg, place):
    g1, g2, rows, width, _, _ = cfg
    shape = (g2 * rows, width)
    spot = lax.broadcasted_iota(jnp.int32, shape, 0)
    col = lax.broadcasted_iota(jnp.int32, shape, 1)
    owner = jnp.bitwise_xor(place[0], turned(place[1], spot >> log2(rows), log2(g2)) * g1)
    return jnp.where(col == owner * rows + (spot & (rows - 1)), 1.0, 0.0).astype(BF)


def fill_side(cfg, place, mask_s, mask_v, w_ref, v_ref, blocks, step, first, outs):
    g1, g2, rows, width, chans, _ = cfg
    z_s, val_s, tan_s, sig_s, gate_s, *zp_s = outs
    if zp_s:
        pick = picker(cfg, place)
    blk = rows * width
    bits = log2(g1 if step == 1 else g2)
    for m, ref in blocks:
        here = slice(m * blk, (m + 1) * blk)
        value = centre(ref[...].reshape(blk, chans).astype(F32))
        zn = (value * scale_of(value)).astype(BF)
        z_s[:, here] = zn.T
        for r in range(rows if zp_s else 0):
            i = m * rows + r
            pairs = dot(pick, zn[r * width : (r + 1) * width]).astype(BF)
            zp_s[0][i * g2 * rows : (i + 1) * g2 * rows, :] = pairs
        proj = dot(zn, w_ref[:, first : first + 2 * chans])
        tang = dot(zn, v_ref[:, first : first + 2 * chans])
        base = jnp.bitwise_xor(place[0], turned(place[1], m, bits) * step) * rows
        cover = jnp.concatenate(
            [mask_v[...] * mask_s[0, base + r].astype(F32) for r in range(rows)], axis=0
        )
        sig = sigmoid(proj[:, chans:])
        held = cover * sig
        val = held * proj[:, :chans]
        gate = val - val * sig
        val_s[here, :] = val.astype(val_s.dtype)
        tan_s[here, :] = (held * tang[:, :chans] + gate * tang[:, chans:]).astype(tan_s.dtype)
        sig_s[here, :] = held.astype(sig_s.dtype)
        gate_s[here, :] = gate.astype(gate_s.dtype)


def own_kernel(cfg, place, mask_s, mask_v, w_ref, v_ref, own_ref, far_ref, *outs):
    g1, chans = cfg[0], cfg[4]
    fill_side(cfg, place, mask_s, mask_v, w_ref, v_ref, [(0, own_ref), (g1 - 1, far_ref)], 1, 0, outs[:6])
    fill_side(cfg, place, mask_s, mask_v, w_ref, v_ref, [(0, own_ref)], g1, 2 * chans, outs[6:])


def triangle(cfg, first, count, a_s, ta_s, b_s, tb_s, px_s, pt_s, x_ref, tx_ref):
    _, g2, rows, width, chans, _ = cfg
    n_j = g2 * rows

    def fold(value):
        return jnp.sum(value.reshape(width // 8, 8, chans), axis=0)

    def tri(i, carry):
        at = pl.ds(pl.multiple_of((first + i) * width, width), width)
        a, ta = a_s[at, :].astype(F32), ta_s[at, :].astype(F32)
        for j in range(n_j):
            here = slice(j * width, (j + 1) * width)
            b, tb = b_s[here, :].astype(F32), tb_s[here, :].astype(F32)
            to = pl.ds(pl.multiple_of(i * (n_j * 8), 8) + j * 8, 8)
            px_s[to, :] = fold(a * b)
            pt_s[to, :] = fold(ta * b + a * tb)
        return carry

    lax.fori_loop(0, count, tri, 0, unroll=4 if width <= 64 else 1)
    pairs = count * n_j
    here = slice(first * n_j, (first + count) * n_j)
    for part, out in ((px_s, x_ref), (pt_s, tx_ref)):
        total = sum(part[pl.ds(s, pairs, stride=8), :] for s in range(8))
        out[here, :] = total.astype(BF).astype(F32)


def line_kernel(cfg, place, mask_s, mask_v, w_ref, v_ref, a_s, ta_s, *rest):
    g1, g2, rows, width, chans, _ = cfg
    refs, (*outs, x_ref, tx_ref, px_s, pt_s) = rest[: g2 - 1], rest[g2 + 4 :]
    fill_side(cfg, place, mask_s, mask_v, w_ref, v_ref,
              [(m + 1, refs[m]) for m in range(g2 - 1)], g1, 2 * chans, outs)
    triangle(cfg, 0, rows, a_s, ta_s, outs[1], outs[2], px_s, pt_s, x_ref, tx_ref)


def block_kernel(cfg, place, mask_s, mask_v, w_ref, v_s, zj_s, b_s, tb_s, sb_s, gb_s, x_in, tx_in, *rest):
    g1, g2, rows, width, chans, total = cfg
    refs = rest[: g1 - 2]
    (keep_ref, send_ref, y_ref, zi_s, a_s, ta_s, sa_s, ga_s, zp_s,
     px_s, pt_s, x_s, tx_s, xb_s, d_s, g_s) = rest[g1 + 4 :]
    n_i, n_j = g1 * rows, g2 * rows
    blk = rows * width
    core = place[1]
    fill_side(cfg, place, mask_s, mask_v, w_ref, v_s,
              [(m, refs[m - 1]) for m in range(g1 - 2, 0, -1)], 1, 0, (zi_s, a_s, ta_s, sa_s, ga_s, zp_s))
    x_s[: rows * n_j, :] = x_in[...]
    tx_s[: rows * n_j, :] = tx_in[...]
    triangle(cfg, rows, n_i - rows, a_s, ta_s, b_s, tb_s, px_s, pt_s, x_s, tx_s)
    pairs = n_i * n_j

    w_gate, w_out = w_ref[:, 4 * chans : 5 * chans], w_ref[:, 5 * chans :]
    v_gate, v_out = v_s[:, 4 * chans : 5 * chans], v_s[:, 5 * chans :]
    step = min(pairs, 128)
    for at in range(0, pairs, step):
        here = slice(at, at + step)
        zp = zp_s[here, :]
        xc = centre(x_s[here, :])
        inv = scale_of(xc)
        xhat = xc * inv
        xn = xhat.astype(BF)
        tc = centre(tx_s[here, :])
        txn = (inv * (tc - xhat * jnp.mean(xhat * tc, axis=1, keepdims=True))).astype(BF)
        out = dot(xn, w_out)
        t_out = dot(txn, w_out) + dot(xn, v_out)
        sig = sigmoid(dot(zp, w_gate))
        slope = sig * (1.0 - sig) * out
        y_ref[here, :] = (sig * out).astype(BF)
        bar = (sig * t_out + slope * dot(zp, v_gate)) * (1.0 / total)
        d_out = (bar * sig).astype(BF)
        d_gate = (bar * slope).astype(BF)
        part_gate = dot(zp, d_gate, ((0,), (0,)))
        part_out = dot(xn, d_out, ((0,), (0,)))
        g_gate = part_gate if at == 0 else g_gate + part_gate
        g_out = part_out if at == 0 else g_out + part_out
        dxn = dot(d_out, w_out, ((1,), (1,)))
        dc = centre(dxn)
        xb_s[here, :] = inv * (dc - xhat * jnp.mean(xhat * dxn, axis=1, keepdims=True))

    g_s[1, chans : 2 * chans, :] = g_gate.astype(BF)
    g_s[1, 2 * chans :, :] = g_out.astype(BF)

    chunk = min(width, 64)

    def back(count, others, row_of, val_s, sig_s, gate_s, z_s, spots):
        def one(m, carry):
            bars = [[] for _ in range(rows)]
            for kc in range(0, width, chunk):
                sums = [None] * rows
                for o in range(others):
                    val = val_s[o * width + kc : o * width + kc + chunk, :].astype(F32)
                    for r in range(rows):
                        term = xb_s[pl.ds(row_of(m * rows + r, o), 1), :] * val
                        sums[r] = term if o == 0 else sums[r] + term
                for r in range(rows):
                    bars[r].append(sums[r])
            bars = sum(bars, [])
            at = pl.ds(pl.multiple_of(m * blk, blk), blk)
            bar = jnp.concatenate(bars, axis=0)
            d_s[at, :chans] = (bar * sig_s[at, :].astype(F32)).astype(BF)
            d_s[at, chans:] = (bar * gate_s[at, :].astype(F32)).astype(BF)
            return carry

        lax.fori_loop(0, count, one, 0, unroll=width <= 64)
        part = dot(z_s[...], d_s[: count * blk, :])
        for n, (half, top) in enumerate(spots):
            g_s[half, top : top + chans, :] = part[:, n * chans : (n + 1) * chans].astype(BF)

    back(g1, n_j, lambda i, j: i * n_j + j, b_s, sa_s, ga_s, zi_s, ((0, 0), (0, chans)))
    back(g2, n_i, lambda j, i: i * n_j + j, a_s, sb_s, gb_s, zj_s, ((0, 2 * chans), (1, 0)))
    keep_ref[...] = g_s[core]
    send_ref[...] = g_s[1 - core]


def pair_kernel(cfg, place, pair_ref, y_ref, new_ref):
    g1, g2, rows, width, _, _ = cfg
    me, core = place[0], place[1]
    n_j = g2 * rows
    col = lax.broadcasted_iota(jnp.int32, (width, width), 0)
    spot = lax.broadcasted_iota(jnp.int32, (width, width), 1)
    n = turned(core, (spot >> log2(rows)) & (g2 - 1), log2(g2))
    s = turned(core, spot >> log2(n_j), log2(g1))
    owner = jnp.bitwise_xor(jnp.bitwise_xor(me, n * g1), s)
    put = jnp.where(col == owner * rows + (spot & (rows - 1)), 1.0, 0.0).astype(BF)
    for r in range(rows):
        y = jnp.concatenate([y_ref[s, r * n_j : (r + 1) * n_j, :] for s in range(g1)], axis=0)
        new_ref[r] = (pair_ref[r].astype(F32) + dot(put, y)).astype(BF)


def shards(pair, crop_mask, weights, probe_signs):
    own = pair[0]
    rows, width, chans = own.shape
    n_axial, n_crop = lax.axis_size("axial"), lax.axis_size("crop")
    g1 = 1 << (log2(n_axial) // 2)
    g2 = n_axial // g1
    n_i, n_j = g1 * rows, g2 * rows
    cfg = (g1, g2, rows, width, chans, n_crop * width * width)

    def crop_swap(value, bit):
        return lax.ppermute(value, "crop", [(i, i ^ bit) for i in range(n_crop)])

    def swap(value, m, step, mixed=True):
        bits = log2(g1 if step == 1 else g2)
        pairs = []
        for q in range(n_crop):
            there = (flip(m, bits) if mixed and q & 1 else m) * step
            pairs += [(q * n_axial + i, q * n_axial + (i ^ there)) for i in range(n_axial)]
        return lax.ppermute(value, ("crop", "axial"), pairs)

    along = [swap(own, m, g1) for m in range(1, g2)]
    place = jnp.stack([lax.axis_index("axial"), lax.axis_index("crop") & 1]).astype(jnp.int32)
    mask_v = jnp.broadcast_to(crop_mask[0].astype(F32)[:, None], (width, chans))
    kept = F32 if width <= 64 else BF
    shape = jax.ShapeDtypeStruct
    pairs = (n_i * n_j, chans)
    side = lambda n: [shape((chans, n * width), BF)] + [shape((n * width, chans), t) for t in (kept,) * 4]
    side_a, side_b = side(n_i) + [shape(pairs, BF)], side(n_j)
    half = shape((3 * chans, chans), BF)
    params = lambda: pltpu.CompilerParams(vmem_limit_bytes=(40 if width <= 64 else 58) << 20)
    cost = lambda us: pl.CostEstimate(flops=int(us * 1e9), bytes_accessed=0, transcendentals=0)

    unit = 1.0 / np.sqrt(np.float32(chans))
    v = ((2 * probe_signs - 1).astype(F32) * unit).astype(BF)
    later, v = lax.optimization_barrier((own, v))
    last, along[-1] = lax.optimization_barrier((later, along[-1]))
    starts = [last] + [later] * (g1 - 3) + [own]
    plane = [swap(starts[m - 1], m, 1) for m in range(1, g1)]
    sides = pl.pallas_call(
        functools.partial(own_kernel, cfg),
        out_shape=side_a + side_b,
        in_specs=[SMEM, SMEM] + [VMEM] * 5,
        out_specs=[VMEM] * 11,
        compiler_params=params(),
        cost_estimate=cost(0.01),
        name="own_rows",
    )(place, crop_mask, mask_v, weights, v, own, plane[-1])
    own_pairs = shape((rows * n_j, chans), F32)
    part = pltpu.VMEM((rows * n_j * 8 + 8, chans), F32)
    *line, x, tx = pl.pallas_call(
        functools.partial(line_kernel, cfg),
        out_shape=side_b + [own_pairs, own_pairs],
        in_specs=[SMEM, SMEM] + [VMEM] * (5 + g2 - 1 + 5),
        out_specs=[VMEM] * 7,
        input_output_aliases={6 + g2 + i: i for i in range(5)},
        scratch_shapes=[part, part],
        compiler_params=params(),
        cost_estimate=cost(0.01),
        name="line",
    )(place, crop_mask, mask_v, weights, v, sides[1], sides[2], *along, *sides[6:])
    part = pltpu.VMEM(((n_i - rows) * n_j * 8 + 8, chans), F32)
    keep, send, y, *_ = pl.pallas_call(
        functools.partial(block_kernel, cfg),
        out_shape=[half, half, shape(pairs, BF)] + side_a,
        in_specs=[SMEM, SMEM] + [VMEM] * (10 + g1 - 2 + 6),
        out_specs=[VMEM] * 9,
        input_output_aliases={10 + g1 + i: 3 + i for i in range(6)},
        scratch_shapes=[part, part]
        + [pltpu.VMEM(pairs, F32)] * 3
        + [pltpu.VMEM((max(n_i, n_j) * width, 2 * chans), BF)]
        + [pltpu.VMEM((2, 3 * chans, chans), BF)],
        compiler_params=params(),
        cost_estimate=cost(5.0),
        name="block",
    )(place, crop_mask, mask_v, weights, v, *line, x, tx, *plane[:-1], *sides[:6])

    def plus(one, two):
        return (one.astype(F32) + two.astype(F32)).astype(BF)

    g = plus(keep, crop_swap(send, 1))
    bit = 2
    while bit < n_crop:
        g = plus(g, crop_swap(g, bit))
        bit *= 2
    y = y.reshape(g1, 1, rows * n_j, chans)
    bit = 1
    while bit < g1:
        parts = y.reshape((y.shape[0] // 2, 2) + y.shape[1:])
        out = parts[:, 1].reshape(-1, chans)
        got = swap(jnp.concatenate([g, out], axis=0), bit, 1)
        g = plus(g, got[: 3 * chans])
        y = jnp.concatenate([parts[:, 0], got[3 * chans :].reshape(parts[:, 1].shape)], axis=1)
        bit *= 2
    new_pair = pl.pallas_call(
        functools.partial(pair_kernel, cfg),
        out_shape=shape(own.shape, BF),
        in_specs=[SMEM] + [VMEM] * 2,
        out_specs=VMEM,
        compiler_params=params(),
        cost_estimate=cost(0.5),
        name="new_pair",
    )(place, own, y[0])
    bit = 1
    while bit < g2:
        g = plus(g, swap(g, bit, g1, False))
        g, new_pair = lax.optimization_barrier((g, new_pair))
        bit *= 2
    other = crop_swap(g, 1)
    first = place[1] == 0
    low, high = jnp.where(first, g, other), jnp.where(first, other, g)
    curvature = jnp.concatenate([p[n * chans : (n + 1) * chans].astype(F32) for p in (low, high) for n in range(3)], axis=1)
    return (new_pair[None], curvature)


def solution(mesh):
    placed = (P("crop", "axial", None, None), P("crop", None), P(), P())
    return jax.shard_map(
        shards,
        mesh=mesh,
        in_specs=placed,
        out_specs=(P("crop", "axial", None, None), P()),
        check_vma=False,
    )
```
